32 devices in a mesh: group: 2 (over y), lender: 4 (over z), tensor: 4 (over x, core).
Axes of the slice: x: 2, y: 2, z: 4, core: 2. Of those that a mesh axis runs over, the one named last changes fastest.
Arguments:
- activations: bfloat16 [16, 8192], P('group', 'lender'), parts along dimension 0, may hold values from -400 to 400
- norm_gain: bfloat16 [8192], P('lender'), may hold values from 0.099609375 to 1.8984375
- w_query: bfloat16 [8192, 8192], P('lender', 'tensor'), may hold values from -0.0625 to 0.0625
- w_out: bfloat16 [8192, 8192], P('tensor', 'lender'), may hold values from -0.0625 to 0.0625
- key_pool: bfloat16 [8, 256, 128, 128], P('tensor', ('group', 'lender')), parts along dimension 1, may hold values from -800 to 800
- value_block_store: bfloat16 [8, 256, 128, 128], P('tensor', ('group', 'lender')), parts along dimension 1, may hold values from -48 to 48
- block_list: int32 [16, 8, 16], P('group', 'tensor'), parts along dimension 0, may hold values from 0 to 127, as said below
- block_slot_table: int32 [8, 256], P('tensor', 'group'), parts along dimension 1, may hold values from 0 to 127, each once within a row
- kept_len: int32 [16, 8], P('group', 'tensor'), parts along dimension 0, may hold values from 1 to 16, as said below
Outputs:
- output: bfloat16 [16, 8192], P(('group', 'tensor'), 'lender'), parts along dimension 0
The draws below stay inside these ranges and needn't reach their ends.
There are 2 independent parts, one for each index of `group`. The reference program is written for one: setup_inputs(seed, part) draws one part's arguments, and reference() takes and returns one part's arrays. A program takes and returns all parts, laid end to end along the dimension named above; an argument that names none is the same for every part. Nothing has to cross between parts.
Inputs may be any that keep to these rules, and one draw needn't show every extreme that they name: `block_list`: for each KV head, no logical block appears twice among all rows' lists. `kept_len`: some row of every KV head keeps 16 blocks and some other row keeps one.
All inputs are finite; a program needn't handle non-finite values.
Results may differ from the reference program's by a relative error of at most 0.012.
The reference program's roundings to bfloat16 on the way count: a program that leaves them out, or rounds other values in their place, can miss the bound.
Values may be sent and summed in bfloat16 or wider, within the bound.
A program may use at most 64 MiB of HBM per device.

```python
import jax
import jax.numpy as jnp
from jax import lax

D = 8192
QUERY_HEADS = 64
KEY_VALUE_HEADS = 8
HEAD_SIZE = 128
BLOCK_TOKENS = 128
DECODED_ROWS = 8
POOL_BLOCKS = 128
KEPT_BLOCKS_MOST = 16


def draw_activations(key, part):
    key_entries, key_cols, key_rows = jax.random.split(jax.random.fold_in(key, 3), 3)
    entries = jax.random.normal(key_entries, (DECODED_ROWS, D), jnp.float32)
    entries = jnp.clip(entries, -6.0, 6.0)
    column_scale = jnp.exp(jnp.log(10.0) * jax.random.uniform(key_cols, (D,), jnp.float32))
    column_scale = column_scale * (1.0 + 2.0 * jnp.arange(D, dtype=jnp.float32) / D)
    row_scale = jnp.exp(jnp.log(10.0) * jax.random.uniform(key_rows, (DECODED_ROWS, 1), jnp.float32))
    return (entries * column_scale * row_scale / 5.0).astype(jnp.bfloat16)


def draw_key_pool(key, part):
    key_noise = jax.random.fold_in(jax.random.fold_in(key, 5), 0)
    full_shape = (KEY_VALUE_HEADS, POOL_BLOCKS, BLOCK_TOKENS, HEAD_SIZE)
    noise_part = jnp.clip(jax.random.normal(key_noise, full_shape, jnp.float32), -4.0, 4.0)
    return noise_part.astype(jnp.bfloat16)


def draw_block_list(key, part):
    keys_per_head = jax.random.split(jax.random.fold_in(key, 11), KEY_VALUE_HEADS)
    shuffled_slots = jax.vmap(lambda head_key: jax.random.permutation(head_key, POOL_BLOCKS))(keys_per_head)
    selected_index = shuffled_slots[:, :DECODED_ROWS * KEPT_BLOCKS_MOST].reshape(KEY_VALUE_HEADS, DECODED_ROWS, KEPT_BLOCKS_MOST)
    return jnp.transpose(selected_index, (1, 0, 2)).astype(jnp.int32)


def draw_kept_len(key, part):
    key_length_draw, key_upper_bound, key_small_scale = jax.random.split(jax.random.fold_in(key, 23), 3)
    row_lengths = jax.random.randint(key_length_draw, (DECODED_ROWS, KEY_VALUE_HEADS), 1, KEPT_BLOCKS_MOST + 1, jnp.int32)
    longest_length = jax.random.randint(key_upper_bound, (1, KEY_VALUE_HEADS), 0, DECODED_ROWS, jnp.int32)
    shortest_length = (longest_length + jax.random.randint(key_small_scale, (1, KEY_VALUE_HEADS), 1, DECODED_ROWS, jnp.int32)) % DECODED_ROWS
    row_ids = jnp.arange(DECODED_ROWS, dtype=jnp.int32)[:, None]
    row_lengths = jnp.where(row_ids == longest_length, KEPT_BLOCKS_MOST, row_lengths)
    row_lengths = jnp.where(row_ids == shortest_length, 1, row_lengths)
    return row_lengths.astype(jnp.int32)


def levels(key, shape, shards, low, top_value):
    def one(axis_at, shards_of):
        draws = jax.random.uniform(jax.random.fold_in(jax.random.fold_in(key, 6), axis_at), (shards_of,), jnp.float32, low / len(shards), top_value / len(shards))
        return jnp.repeat(jnp.exp(draws), shape[axis_at] // shards_of).reshape((-1,) + (1,) * (len(shape) - axis_at - 1))

    loudness = one(*shards[0])
    for cut in shards[1:]:
        loudness = loudness * one(*cut)
    return loudness


def bell_draw(key, shape, spread, bound, cuts=(), kind=jnp.bfloat16):
    values = jax.random.normal(key, shape, jnp.float32) * spread
    if len(cuts) > 0:
        values = levels(key, shape, cuts, -0.22, 0.18) * values
    return jnp.clip(values, min=-bound, max=bound).astype(kind)


def setup_inputs(seed: int = 0, part: int = 0) -> dict:
    key_list = jax.random.split(jax.random.key(seed), 10)
    part_splits = jax.random.split(jax.random.fold_in(key_list[9], part), 10)
    return {
        "activations": draw_activations(jax.random.fold_in(jax.random.fold_in(key_list[9], part), 71), part),
        "norm_gain": jnp.clip(1.0 + 0.18 * jax.random.normal(key_list[1], (D,), jnp.float32), 0.099609375, 1.8984375).astype(jnp.bfloat16),
        "w_query": bell_draw(key_list[2], (D, QUERY_HEADS * HEAD_SIZE), D ** -0.5, 0.0625, ((0, 4), (1, 4))),
        "w_out": bell_draw(key_list[3], (QUERY_HEADS * HEAD_SIZE, D), (QUERY_HEADS * HEAD_SIZE) ** -0.5, 0.0625, ((0, 4), (1, 4))),
        "key_pool": draw_key_pool(jax.random.fold_in(jax.random.fold_in(key_list[9], part), 71), part),
        "value_block_store": bell_draw(part_splits[5], (KEY_VALUE_HEADS, POOL_BLOCKS, BLOCK_TOKENS, HEAD_SIZE), 8.0, 48.0, ((0, 4), (1, 4))),
        "block_list": draw_block_list(jax.random.fold_in(jax.random.fold_in(key_list[9], part), 71), part),
        "block_slot_table": jax.vmap(lambda own: jax.random.permutation(own, POOL_BLOCKS))(jax.random.split(part_splits[7], KEY_VALUE_HEADS)).reshape((KEY_VALUE_HEADS, POOL_BLOCKS)).astype(jnp.int32),
        "kept_len": draw_kept_len(jax.random.fold_in(jax.random.fold_in(key_list[9], part), 71), part),
    }


epsilon = 1e-05

def reference(activations, norm_gain, w_query, w_out, key_pool, value_block_store, block_list, block_slot_table, kept_len):
    features = activations.astype(jnp.float32)
    mean_square = lax.optimization_barrier(jnp.mean(features * features, axis=1))
    scaled = (features * norm_gain.astype(jnp.float32)).astype(jnp.bfloat16)
    projected = jnp.dot(scaled, w_query, preferred_element_type=jnp.float32)
    query_vectors = (projected * lax.rsqrt(mean_square + epsilon)[:, None] * HEAD_SIZE ** (-0.5)).astype(jnp.bfloat16)
    query_vectors = query_vectors.reshape(DECODED_ROWS, KEY_VALUE_HEADS, QUERY_HEADS // KEY_VALUE_HEADS, HEAD_SIZE)
    slot_lookup_table = jnp.broadcast_to(block_slot_table[None], (DECODED_ROWS, KEY_VALUE_HEADS, POOL_BLOCKS))
    slot_ids = jnp.take_along_axis(slot_lookup_table, block_list, axis=2)
    is_live = jnp.arange(KEPT_BLOCKS_MOST, dtype=jnp.int32)[None, None, :] < kept_len[:, :, None]
    kv_head_position = jnp.arange(KEY_VALUE_HEADS, dtype=jnp.int32)[:, None]

    def one_row(packed):
        row_query, row_slots, row_live = packed
        row_keys = key_pool[kv_head_position, row_slots].astype(jnp.float32)
        row_values = value_block_store[kv_head_position, row_slots].astype(jnp.float32)
        scores = jnp.einsum('hgd,hktd->hgkt', row_query.astype(jnp.float32), row_keys)
        scores = jnp.where(row_live[:, None, :, None], scores, -jnp.inf)
        best_score = lax.optimization_barrier(jnp.max(scores, axis=(2, 3), keepdims=True))
        weights_full = jnp.exp(scores - best_score)
        sum_weight = lax.optimization_barrier(jnp.sum(weights_full, axis=(2, 3)))
        rounded = lax.optimization_barrier(weights_full.astype(jnp.bfloat16)).astype(jnp.float32)
        sum_value = jnp.einsum('hgkt,hktd->hgd', rounded, row_values)
        return (sum_value / sum_weight[..., None]).astype(jnp.bfloat16)
    attended = lax.map(one_row, (query_vectors, slot_ids, is_live))
    attended = attended.reshape(DECODED_ROWS, QUERY_HEADS * HEAD_SIZE)
    return jnp.dot(attended, w_out, preferred_element_type=jnp.float32).astype(jnp.bfloat16)
```

```python
import functools

import jax
import jax.numpy as jnp
from jax import lax
from jax.experimental import pallas as pl
from jax.experimental.pallas import tpu as pltpu
from jax.sharding import PartitionSpec as P

very_low = -1e30
epsilon = 1e-05


def separate_ops(
    activations,
    norm_gain,
    w_query,
    w_out,
    key_pool,
    value_block_store,
    block_list,
    block_slot_table,
    kept_len,
):
    row_count = activations.shape[0]
    kv_heads = key_pool.shape[0]
    slot_count = key_pool.shape[1]
    head_dim = key_pool.shape[3]
    kept_most = block_list.shape[2]
    features = activations.astype(jnp.float32)
    squares = jnp.sum(features * features, axis=1)
    scaled = (features * norm_gain.astype(jnp.float32)).astype(jnp.bfloat16)
    partial_value = jnp.dot(scaled, w_query, preferred_element_type=jnp.float32)
    projected, square_sum = lax.psum((partial_value, squares), "lender")
    width = features.shape[1] * lax.axis_size("lender")
    inverse = lax.rsqrt(square_sum / width + epsilon)
    query_vectors = (projected * inverse[:, None] * head_dim ** (-0.5)).astype(jnp.bfloat16)
    group_size = query_vectors.shape[1] // (kv_heads * head_dim)
    query_vectors = query_vectors.reshape(row_count, kv_heads, group_size, head_dim)
    slot_lookup_table = jnp.broadcast_to(
        block_slot_table[None], (row_count,) + block_slot_table.shape
    )
    slot_ids = jnp.take_along_axis(slot_lookup_table, block_list, axis=2)
    positions = jnp.arange(kept_most, dtype=jnp.int32)
    is_live = positions[None, None, :] < kept_len[:, :, None]
    local_slot = slot_ids - lax.axis_index("lender") * slot_count
    matches = is_live[..., None] & (
        local_slot[..., None] == jnp.arange(slot_count, dtype=jnp.int32)
    )
    owner_mask = jnp.transpose(jnp.any(matches, axis=2), (1, 2, 0))
    owner_half = owner_mask.astype(jnp.bfloat16)
    owner_full = owner_mask.astype(jnp.float32)
    used_slot = jnp.any(owner_mask, axis=2)
    picked = jnp.einsum(
        "hsr,rhgd->hsgd", owner_half, query_vectors, preferred_element_type=jnp.float32
    ).astype(jnp.bfloat16)
    scores = jnp.einsum("hsgd,hstd->hsgt", picked, key_pool, preferred_element_type=jnp.float32)
    block_best = jnp.max(scores, axis=3)
    spread = jnp.where(owner_mask[..., None], block_best[:, :, None, :], very_low)
    row_best = jnp.max(spread, axis=1)
    slot_best = jnp.max(jnp.where(owner_mask[..., None], row_best[:, None, :, :], very_low), axis=2)
    slot_best = jnp.where(used_slot[..., None], slot_best, 0.0)
    weights_full = jnp.where(
        used_slot[:, :, None, None], jnp.exp(scores - slot_best[..., None]), 0.0
    )
    slot_weight = jnp.sum(weights_full, axis=3)
    slot_value = jnp.einsum(
        "hsgt,hstd->hsgd",
        weights_full.astype(jnp.bfloat16),
        value_block_store,
        preferred_element_type=jnp.float32,
    )
    row_weight = jnp.einsum(
        "hsr,hsg->rhg", owner_full, slot_weight, precision=lax.Precision.HIGHEST
    )
    row_value = jnp.einsum(
        "hsr,hsgd->rhgd", owner_full, slot_value, precision=lax.Precision.HIGHEST
    )
    row_high = jnp.transpose(row_best, (1, 0, 2))
    lenders = lax.axis_size("lender")
    home_rows = row_count // lenders
    came_best, came_weight, came_value = (
        lax.all_to_all(row_high, "lender", split_axis=0, concat_axis=0, tiled=True),
        lax.all_to_all(row_weight, "lender", split_axis=0, concat_axis=0, tiled=True),
        lax.all_to_all(row_value, "lender", split_axis=0, concat_axis=0, tiled=True),
    )
    came_best = came_best.reshape((lenders, home_rows) + came_best.shape[1:])
    came_weight = came_weight.reshape((lenders, home_rows) + came_weight.shape[1:])
    came_value = came_value.reshape((lenders, home_rows) + came_value.shape[1:])
    highest = jnp.max(came_best, axis=0)
    factor = jnp.exp(came_best - highest[None])
    home_weight = jnp.sum(came_weight * factor, axis=0)
    home_value = jnp.sum(came_value * factor[..., None], axis=0)
    home_attended = (
        (home_value / home_weight[..., None]).astype(jnp.bfloat16).reshape(home_rows, -1)
    )
    attended = lax.all_gather(home_attended, "lender", axis=0, tiled=True)
    result = lax.psum_scatter(
        jnp.dot(attended, w_out, preferred_element_type=jnp.float32),
        "tensor",
        scatter_dimension=0,
        tiled=True,
    )
    return result.astype(jnp.bfloat16)


MESH = pl.DeviceIdType.MESH
LANES = 128
SUBLANES = 8


def fused_kernel(
    lenders,
    tensors,
    act_ref,
    gain_ref,
    list_ref,
    table_ref,
    kept_ref,
    wq_hbm,
    wo_hbm,
    key_hbm,
    value_hbm,
    out_ref,
    wq,
    wo,
    keys,
    values,
    q_send,
    q_recv,
    q_all,
    bias,
    scores,
    part_send,
    part_recv,
    att_all,
    sum_send,
    sum_recv,
    wq_sem,
    wo_sem,
    kv_sem,
    lender_send,
    lender_recv,
    tensor_send,
    tensor_recv,
):
    me = lax.axis_index("lender")
    mine = lax.axis_index("tensor")
    rows = act_ref.shape[0]
    kv_heads, slot_count, tokens, head_dim = keys.shape
    width = wq.shape[2]
    chunk_heads = width // head_dim
    chunk_rows = chunk_heads * rows
    group = wo.shape[0] * chunk_heads // kv_heads
    chunks_per_kv = group // chunk_heads
    kept_most = list_ref.shape[1] // kv_heads
    f32, bf16 = jnp.float32, jnp.bfloat16

    def lender_at(offset):
        return lax.rem(me + offset, lenders)

    wq_copies = []
    for offset in list(range(1, lenders)) + [0]:
        columns = pl.ds(pl.multiple_of(lender_at(offset) * width, width), width)
        wq_copies.append(
            pltpu.make_async_copy(wq_hbm.at[:, columns], wq.at[offset], wq_sem.at[offset])
        )
    key_copy = pltpu.make_async_copy(key_hbm, keys, kv_sem.at[0])
    value_copy = pltpu.make_async_copy(value_hbm, values, kv_sem.at[1])
    wo_copies = []
    for offset in range(lenders):
        source = lender_at(lenders - offset)
        lines = pl.ds(pl.multiple_of(source * width, width), width)
        wo_copies.append(
            pltpu.make_async_copy(wo_hbm.at[lines], wo.at[offset], wo_sem.at[offset])
        )
    for copy in wq_copies:
        copy.start()

    barrier = pltpu.get_barrier_semaphore()
    for offset in range(1, lenders):
        pl.semaphore_signal(
            barrier, inc=1, device_id={"lender": lender_at(offset)}, device_id_type=MESH
        )
    for offset in range(1, tensors):
        pl.semaphore_signal(
            barrier,
            inc=1,
            device_id={"tensor": lax.rem(mine + offset, tensors)},
            device_id_type=MESH,
        )

    def to_lender(stage, offset, src, dst):
        return pltpu.make_async_remote_copy(
            src_ref=src,
            dst_ref=dst,
            send_sem=lender_send.at[stage, offset],
            recv_sem=lender_recv.at[stage, offset],
            device_id={"lender": lender_at(offset)},
            device_id_type=MESH,
        )

    features = act_ref[...].astype(f32)
    squares = jnp.sum(features * features, axis=1, keepdims=True)
    scaled = (features * gain_ref[...].astype(f32)).astype(bf16)

    blocks = table_ref.shape[1]
    block_ids = lax.broadcasted_iota(jnp.int32, (rows, blocks), 1)
    local_slots = lax.broadcasted_iota(jnp.int32, (slot_count, blocks), 0) + me * slot_count
    for h in range(kv_heads):
        member = jnp.zeros((rows, blocks), f32)
        for k in range(kept_most):
            at = h * kept_most + k
            hit = (list_ref[:, at : at + 1] == block_ids) & (kept_ref[:, h : h + 1] > k)
            member = jnp.where(hit, 1.0, member)
        holds = jnp.where(table_ref[h : h + 1, :] == local_slots, 1.0, 0.0)
        owner = lax.dot_general(
            member.astype(bf16),
            holds.astype(bf16),
            (((1,), (1,)), ((), ())),
            preferred_element_type=f32,
        )
        lowered = (owner - 1.0) * -very_low
        for s in range(slot_count):
            bias[h, :, s * tokens : (s + 1) * tokens] = jnp.broadcast_to(
                lowered[:, s : s + 1], (rows, tokens)
            )

    started = []
    own_partial = None
    for at, offset in enumerate(list(range(1, lenders)) + [0]):
        wq_copies[at].wait()
        if at == 0:
            key_copy.start()
            value_copy.start()
        if at == min(1, lenders - 1):
            for copy in wo_copies:
                copy.start()
        partial = jnp.dot(scaled, wq[offset], preferred_element_type=f32)
        if offset == 0:
            own_partial = partial
            continue
        q_send[offset, :, :width] = partial
        q_send[offset, :, width:] = jnp.broadcast_to(squares, (rows, LANES))
        if at == 0:
            pl.semaphore_wait(barrier, lenders + tensors - 2)
        copy = to_lender(0, offset, q_send.at[offset], q_recv.at[offset])
        copy.start()
        started.append(copy)

    projected, square_sum = own_partial, squares
    for copy in started:
        copy.wait_recv()
    for offset in range(1, lenders):
        projected = projected + q_recv[offset, :, :width]
        square_sum = square_sum + q_recv[offset, :, width : width + 1]
    inverse = lax.rsqrt(square_sum / (act_ref.shape[1] * lenders) + epsilon)
    normed = projected * inverse * head_dim ** (-0.5)
    q_all[me] = jnp.concatenate(
        [normed[:, j * head_dim : (j + 1) * head_dim] for j in range(chunk_heads)], axis=0
    ).astype(bf16)
    q_copies = []
    for offset in range(1, lenders):
        copy = to_lender(1, offset, q_all.at[me], q_all.at[me])
        copy.start()
        q_copies.append(copy)
    key_copy.wait()
    for copy in q_copies:
        copy.wait_recv()
    started += q_copies

    step_slots = max(1, min(slot_count, 512 // tokens))
    step = step_slots * tokens
    steps = slot_count // step_slots
    high = []
    for h in range(kv_heads):
        queries = q_all[h * chunks_per_kv : (h + 1) * chunks_per_kv].reshape(
            group * rows, head_dim
        )
        running = None
        for c in range(steps):
            block = keys[h, c * step_slots : (c + 1) * step_slots].reshape(step, head_dim)
            found = lax.dot_general(
                queries, block, (((1,), (1,)), ((), ())), preferred_element_type=f32
            )
            found = found.reshape(group, rows, step) + bias[h, :, c * step : (c + 1) * step][None]
            found = found.reshape(group * rows, step)
            scores[h, :, c * step : (c + 1) * step] = found
            for t in range(0, step, LANES):
                piece = found[:, t : t + LANES]
                running = piece if running is None else jnp.maximum(running, piece)
        high.append(jnp.max(running, axis=1, keepdims=True))
    value_copy.wait()

    eye = lax.broadcasted_iota(jnp.int32, (chunk_rows, LANES), 0) == lax.broadcasted_iota(
        jnp.int32, (chunk_rows, LANES), 1
    )
    first_line = lax.broadcasted_iota(jnp.int32, (SUBLANES, LANES), 0) == 0
    for h in range(kv_heads):
        best = high[h]
        total = None
        gathered = jnp.zeros((group * rows, head_dim), f32)
        for c in range(steps):
            weights = jnp.exp(scores[h, :, c * step : (c + 1) * step] - best)
            for t in range(0, step, LANES):
                piece = weights[:, t : t + LANES]
                total = piece if total is None else total + piece
            block = values[h, c * step_slots : (c + 1) * step_slots].reshape(step, head_dim)
            gathered = gathered + jnp.dot(
                weights.astype(bf16), block, preferred_element_type=f32
            )
        total = jnp.sum(total, axis=1, keepdims=True)
        for j in range(chunks_per_kv):
            lines = slice(j * chunk_rows, (j + 1) * chunk_rows)
            d = h * chunks_per_kv + j
            best_line = jnp.sum(jnp.where(eye, best[lines], 0.0), axis=0, keepdims=True)
            total_line = jnp.sum(jnp.where(eye, total[lines], 0.0), axis=0, keepdims=True)
            part_send[d, :chunk_rows, :] = gathered[lines]
            part_send[d, chunk_rows:, :] = jnp.where(first_line, best_line, total_line)

    part_copies = []
    for offset in range(1, lenders):
        copy = to_lender(2, offset, part_send.at[lender_at(offset)], part_recv.at[offset])
        copy.start()
        part_copies.append(copy)
    started += part_copies
    part_recv[0] = part_send[me]
    for copy in part_copies:
        copy.wait_recv()
    bests, totals = [], []
    for offset in range(lenders):
        line = part_recv[offset, chunk_rows : chunk_rows + 1, :]
        bests.append(jnp.sum(jnp.where(eye, line, 0.0), axis=1, keepdims=True))
        line = part_recv[offset, chunk_rows + 1 : chunk_rows + 2, :]
        totals.append(jnp.sum(jnp.where(eye, line, 0.0), axis=1, keepdims=True))
    highest = functools.reduce(jnp.maximum, bests)
    home_total = jnp.zeros((chunk_rows, 1), f32)
    home_value = jnp.zeros((chunk_rows, head_dim), f32)
    for offset in range(lenders):
        factor = jnp.exp(bests[offset] - highest)
        home_total = home_total + totals[offset] * factor
        home_value = home_value + part_recv[offset, :chunk_rows, :] * factor
    att_all[me] = (home_value / home_total).astype(bf16)
    att_copies = []
    for offset in range(1, lenders):
        copy = to_lender(3, offset, att_all.at[me], att_all.at[me])
        copy.start()
        att_copies.append(copy)
    started += att_copies

    product = None
    for offset in range(lenders):
        wo_copies[offset].wait()
        if offset > 0:
            att_copies[offset - 1].wait_recv()
        chunk = att_all[lender_at(lenders - offset)].astype(f32)
        chunk = jnp.concatenate(
            [chunk[j * rows : (j + 1) * rows] for j in range(chunk_heads)], axis=1
        ).astype(bf16)
        term = jnp.dot(chunk, wo[offset], preferred_element_type=f32)
        product = term if product is None else product + term

    home_rows = rows // tensors
    part_width = product.shape[1] // tensors
    line_block = lax.broadcasted_iota(jnp.int32, (rows, part_width), 0) // home_rows
    for d in range(tensors):
        packed = jnp.zeros((rows, part_width), f32)
        for c in range(tensors):
            piece = product[:, c * part_width : (c + 1) * part_width]
            shift = (c - d) * home_rows % rows
            if shift:
                piece = pltpu.roll(piece, shift, 0)
            packed = jnp.where(line_block == c, piece, packed)
        sum_send[d] = packed
    for offset in range(1, tensors):
        target = lax.rem(mine + offset, tensors)
        copy = pltpu.make_async_remote_copy(
            src_ref=sum_send.at[target],
            dst_ref=sum_recv.at[offset],
            send_sem=tensor_send.at[offset],
            recv_sem=tensor_recv.at[offset],
            device_id={"tensor": target},
            device_id_type=MESH,
        )
        copy.start()
        started.append(copy)
    result = sum_send[mine]
    for copy in started[1 - tensors :] if tensors > 1 else []:
        copy.wait_recv()
    for offset in range(1, tensors):
        result = result + sum_recv[offset]
    for c in range(tensors):
        out_ref[:, c * part_width : (c + 1) * part_width] = result[
            c * home_rows : (c + 1) * home_rows
        ].astype(out_ref.dtype)
    for copy in started:
        copy.wait_send()


def fused(
    activations,
    norm_gain,
    w_query,
    w_out,
    key_pool,
    value_block_store,
    block_list,
    block_slot_table,
    kept_len,
):
    lenders, tensors = lax.axis_size("lender"), lax.axis_size("tensor")
    rows, depth = activations.shape
    kv_heads, slot_count, tokens, head_dim = key_pool.shape
    width = w_query.shape[1] // lenders
    out_width = w_out.shape[1]
    chunk_rows = width // head_dim * rows
    group_rows = w_query.shape[1] // head_dim // kv_heads * rows
    part_width = out_width // tensors
    f32, bf16 = jnp.float32, jnp.bfloat16
    vmem = pl.BlockSpec(memory_space=pltpu.VMEM)
    hbm = pl.BlockSpec(memory_space=pl.ANY)
    return pl.pallas_call(
        functools.partial(fused_kernel, lenders, tensors),
        out_shape=jax.ShapeDtypeStruct((rows // tensors, out_width), bf16),
        in_specs=[vmem] * 5 + [hbm] * 4,
        out_specs=vmem,
        scratch_shapes=[
            pltpu.VMEM((lenders, depth, width), bf16),
            pltpu.VMEM((lenders, width, out_width), bf16),
            pltpu.VMEM(key_pool.shape, bf16),
            pltpu.VMEM(key_pool.shape, bf16),
            pltpu.VMEM((lenders, rows, width + LANES), f32),
            pltpu.VMEM((lenders, rows, width + LANES), f32),
            pltpu.VMEM((lenders, chunk_rows, head_dim), bf16),
            pltpu.VMEM((kv_heads, rows, slot_count * tokens), f32),
            pltpu.VMEM((kv_heads, group_rows, slot_count * tokens), f32),
            pltpu.VMEM((lenders, chunk_rows + SUBLANES, head_dim), f32),
            pltpu.VMEM((lenders, chunk_rows + SUBLANES, head_dim), f32),
            pltpu.VMEM((lenders, chunk_rows, head_dim), bf16),
            pltpu.VMEM((tensors, rows, part_width), f32),
            pltpu.VMEM((tensors, rows, part_width), f32),
            pltpu.SemaphoreType.DMA((lenders,)),
            pltpu.SemaphoreType.DMA((lenders,)),
            pltpu.SemaphoreType.DMA((2,)),
            pltpu.SemaphoreType.DMA((4, lenders)),
            pltpu.SemaphoreType.DMA((4, lenders)),
            pltpu.SemaphoreType.DMA((tensors,)),
            pltpu.SemaphoreType.DMA((tensors,)),
        ],
        compiler_params=pltpu.CompilerParams(
            collective_id=0, has_side_effects=True, vmem_limit_bytes=48 * 2**20
        ),
        name="decode_attention",
    )(
        activations,
        norm_gain[None],
        block_list.reshape(rows, -1),
        block_slot_table,
        kept_len,
        w_query,
        w_out,
        key_pool,
        value_block_store,
    )


def per_device(*arrays):
    activations, _, w_query, w_out, key_pool = arrays[:5]
    lenders, tensors = lax.axis_size("lender"), lax.axis_size("tensor")
    rows = activations.shape[0]
    kv_heads, slot_count, tokens, head_dim = key_pool.shape
    columns, out_width = w_query.shape[1], w_out.shape[1]
    width = columns // lenders
    fits = (
        rows == SUBLANES
        and head_dim == LANES
        and tokens == LANES
        and columns % (lenders * head_dim) == 0
        and columns // kv_heads % max(width, 1) == 0
        and width * rows % (2 * SUBLANES * head_dim) == 0
        and width * rows <= LANES * head_dim
        and rows % tensors == 0
        and out_width % (tensors * LANES) == 0
        and slot_count * tokens % 512 == 0
    )
    return (fused if fits else separate_ops)(*arrays)


def solution(mesh):
    in_specs = (
        P("group", "lender"),
        P("lender"),
        P("lender", "tensor"),
        P("tensor", "lender"),
        P("tensor", ("group", "lender"), None, None),
        P("tensor", ("group", "lender"), None, None),
        P("group", "tensor", None),
        P("tensor", "group"),
        P("group", "tensor"),
    )
    out_specs = P(("group", "tensor"), "lender")
    return jax.shard_map(
        per_device, mesh=mesh, in_specs=in_specs, out_specs=out_specs, check_vma=False
    )
```

```python
import functools

import jax
import jax.numpy as jnp
from jax import lax
from jax.experimental import pallas as pl
from jax.experimental.pallas import tpu as pltpu
from jax.sharding import PartitionSpec as P

very_low = -1e30
epsilon = 1e-05


def separate_ops(
    activations,
    norm_gain,
    w_query,
    w_out,
    key_pool,
    value_block_store,
    block_list,
    block_slot_table,
    kept_len,
):
    row_count = activations.shape[0]
    kv_heads = key_pool.shape[0]
    slot_count = key_pool.shape[1]
    head_dim = key_pool.shape[3]
    kept_most = block_list.shape[2]
    features = activations.astype(jnp.float32)
    squares = jnp.sum(features * features, axis=1)
    scaled = (features * norm_gain.astype(jnp.float32)).astype(jnp.bfloat16)
    partial_value = jnp.dot(scaled, w_query, preferred_element_type=jnp.float32)
    projected, square_sum = lax.psum((partial_value, squares), "lender")
    width = features.shape[1] * lax.axis_size("lender")
    inverse = lax.rsqrt(square_sum / width + epsilon)
    query_vectors = (projected * inverse[:, None] * head_dim ** (-0.5)).astype(jnp.bfloat16)
    group_size = query_vectors.shape[1] // (kv_heads * head_dim)
    query_vectors = query_vectors.reshape(row_count, kv_heads, group_size, head_dim)
    slot_lookup_table = jnp.broadcast_to(
        block_slot_table[None], (row_count,) + block_slot_table.shape
    )
    slot_ids = jnp.take_along_axis(slot_lookup_table, block_list, axis=2)
    positions = jnp.arange(kept_most, dtype=jnp.int32)
    is_live = positions[None, None, :] < kept_len[:, :, None]
    local_slot = slot_ids - lax.axis_index("lender") * slot_count
    matches = is_live[..., None] & (
        local_slot[..., None] == jnp.arange(slot_count, dtype=jnp.int32)
    )
    owner_mask = jnp.transpose(jnp.any(matches, axis=2), (1, 2, 0))
    owner_half = owner_mask.astype(jnp.bfloat16)
    owner_full = owner_mask.astype(jnp.float32)
    used_slot = jnp.any(owner_mask, axis=2)
    picked = jnp.einsum(
        "hsr,rhgd->hsgd", owner_half, query_vectors, preferred_element_type=jnp.float32
    ).astype(jnp.bfloat16)
    scores = jnp.einsum("hsgd,hstd->hsgt", picked, key_pool, preferred_element_type=jnp.float32)
    block_best = jnp.max(scores, axis=3)
    spread = jnp.where(owner_mask[..., None], block_best[:, :, None, :], very_low)
    row_best = jnp.max(spread, axis=1)
    slot_best = jnp.max(jnp.where(owner_mask[..., None], row_best[:, None, :, :], very_low), axis=2)
    slot_best = jnp.where(used_slot[..., None], slot_best, 0.0)
    weights_full = jnp.where(
        used_slot[:, :, None, None], jnp.exp(scores - slot_best[..., None]), 0.0
    )
    slot_weight = jnp.sum(weights_full, axis=3)
    slot_value = jnp.einsum(
        "hsgt,hstd->hsgd",
        weights_full.astype(jnp.bfloat16),
        value_block_store,
        preferred_element_type=jnp.float32,
    )
    row_weight = jnp.einsum(
        "hsr,hsg->rhg", owner_full, slot_weight, precision=lax.Precision.HIGHEST
    )
    row_value = jnp.einsum(
        "hsr,hsgd->rhgd", owner_full, slot_value, precision=lax.Precision.HIGHEST
    )
    row_high = jnp.transpose(row_best, (1, 0, 2))
    lenders = lax.axis_size("lender")
    home_rows = row_count // lenders
    came_best, came_weight, came_value = (
        lax.all_to_all(row_high, "lender", split_axis=0, concat_axis=0, tiled=True),
        lax.all_to_all(row_weight, "lender", split_axis=0, concat_axis=0, tiled=True),
        lax.all_to_all(row_value, "lender", split_axis=0, concat_axis=0, tiled=True),
    )
    came_best = came_best.reshape((lenders, home_rows) + came_best.shape[1:])
    came_weight = came_weight.reshape((lenders, home_rows) + came_weight.shape[1:])
    came_value = came_value.reshape((lenders, home_rows) + came_value.shape[1:])
    highest = jnp.max(came_best, axis=0)
    factor = jnp.exp(came_best - highest[None])
    home_weight = jnp.sum(came_weight * factor, axis=0)
    home_value = jnp.sum(came_value * factor[..., None], axis=0)
    home_attended = (
        (home_value / home_weight[..., None]).astype(jnp.bfloat16).reshape(home_rows, -1)
    )
    attended = lax.all_gather(home_attended, "lender", axis=0, tiled=True)
    result = lax.psum_scatter(
        jnp.dot(attended, w_out, preferred_element_type=jnp.float32),
        "tensor",
        scatter_dimension=0,
        tiled=True,
    )
    return result.astype(jnp.bfloat16)


MESH = pl.DeviceIdType.MESH
LANES = 128
SUBLANES = 8


def fused_kernel(
    lenders,
    tensors,
    act_hbm,
    gain_hbm,
    list_hbm,
    table_hbm,
    kept_hbm,
    wq_hbm,
    wo_hbm,
    key_hbm,
    value_hbm,
    out_ref,
    act_ref,
    gain_ref,
    list_ref,
    table_ref,
    kept_ref,
    wq,
    wo,
    keys,
    values,
    q_send,
    q_recv,
    q_all,
    bias,
    scores,
    part_send,
    part_recv,
    att_all,
    sum_send,
    sum_recv,
    small_sem,
    wq_sem,
    wo_sem,
    kv_sem,
    lender_send,
    lender_recv,
    tensor_send,
    tensor_recv,
):
    me = lax.axis_index("lender")
    mine = lax.axis_index("tensor")
    rows = act_ref.shape[0]
    kv_heads, slot_count, tokens, head_dim = keys.shape
    width = wq.shape[2]
    chunk_heads = width // head_dim
    chunk_rows = chunk_heads * rows
    group = wo.shape[0] * chunk_heads // kv_heads
    chunks_per_kv = group // chunk_heads
    kept_most = list_ref.shape[2]
    f32, bf16 = jnp.float32, jnp.bfloat16

    def lender_at(offset):
        return lax.rem(me + offset, lenders)

    far_first = sorted(range(1, lenders), key=lambda offset: abs(2 * offset - lenders))
    small_copies = [
        pltpu.make_async_copy(src, dst, small_sem.at[at])
        for at, (src, dst) in enumerate(
            (
                (act_hbm, act_ref),
                (gain_hbm, gain_ref),
                (list_hbm, list_ref),
                (table_hbm, table_ref),
                (kept_hbm, kept_ref),
            )
        )
    ]
    wq_copies = []
    for offset in far_first + [0]:
        columns = pl.ds(pl.multiple_of(lender_at(offset) * width, width), width)
        wq_copies.append(
            pltpu.make_async_copy(wq_hbm.at[:, columns], wq.at[offset], wq_sem.at[offset])
        )
    key_copy = pltpu.make_async_copy(key_hbm, keys, kv_sem.at[0])
    value_copy = pltpu.make_async_copy(value_hbm, values, kv_sem.at[1])
    wo_copies = []
    for offset in range(lenders):
        source = lender_at(lenders - offset)
        lines = pl.ds(pl.multiple_of(source * width, width), width)
        wo_copies.append(
            pltpu.make_async_copy(wo_hbm.at[lines], wo.at[offset], wo_sem.at[offset])
        )
    for copy in small_copies[:2]:
        copy.start()
    for copy in wq_copies:
        copy.start()

    barrier = pltpu.get_barrier_semaphore()
    for offset in range(1, lenders):
        pl.semaphore_signal(
            barrier, inc=1, device_id={"lender": lender_at(offset)}, device_id_type=MESH
        )
    for offset in range(1, tensors):
        pl.semaphore_signal(
            barrier,
            inc=1,
            device_id={"tensor": lax.rem(mine + offset, tensors)},
            device_id_type=MESH,
        )

    def to_lender(stage, offset, src, dst):
        return pltpu.make_async_remote_copy(
            src_ref=src,
            dst_ref=dst,
            send_sem=lender_send.at[stage, offset],
            recv_sem=lender_recv.at[stage, offset],
            device_id={"lender": lender_at(offset)},
            device_id_type=MESH,
        )

    for copy in small_copies[:2]:
        copy.wait()
    features = act_ref[...].astype(f32)
    squares = jnp.sum(features * features, axis=1, keepdims=True)
    scaled = (features * gain_ref[...].astype(f32).reshape(1, -1)).astype(bf16)

    started = []
    own_partial = None
    for at, offset in enumerate(far_first + [0]):
        wq_copies[at].wait()
        if at == 0:
            for copy in small_copies[2:]:
                copy.start()
            key_copy.start()
            value_copy.start()
        if at == min(1, lenders - 1):
            for copy in wo_copies:
                copy.start()
        partial = jnp.dot(scaled, wq[offset], preferred_element_type=f32)
        if offset == 0:
            own_partial = partial
            continue
        q_send[offset, :, :width] = partial
        q_send[offset, :, width:] = jnp.broadcast_to(squares, (rows, LANES))
        if at == 0:
            pl.semaphore_wait(barrier, lenders + tensors - 2)
        copy = to_lender(0, offset, q_send.at[offset], q_recv.at[offset])
        copy.start()
        started.append(copy)

    for copy in small_copies[2:]:
        copy.wait()
    blocks = table_ref.shape[1]
    block_ids = lax.broadcasted_iota(jnp.int32, (rows, blocks), 1)
    local_slots = lax.broadcasted_iota(jnp.int32, (slot_count, blocks), 0) + me * slot_count
    row_eye = lax.broadcasted_iota(jnp.int32, (rows, rows), 0) == lax.broadcasted_iota(
        jnp.int32, (rows, rows), 1
    )
    for h in range(kv_heads):
        member = jnp.zeros((rows, blocks), f32)
        listed = list_ref[:, h, :]
        kept = jnp.sum(jnp.where(row_eye, kept_ref[h : h + 1, :], 0), axis=1, keepdims=True)
        for k in range(kept_most):
            hit = (listed[:, k : k + 1] == block_ids) & (kept > k)
            member = jnp.where(hit, 1.0, member)
        holds = jnp.where(table_ref[h : h + 1, :] == local_slots, 1.0, 0.0)
        owner = lax.dot_general(
            member.astype(bf16),
            holds.astype(bf16),
            (((1,), (1,)), ((), ())),
            preferred_element_type=f32,
        )
        lowered = (owner - 1.0) * -very_low
        for s in range(slot_count):
            bias[h, :, s * tokens : (s + 1) * tokens] = jnp.broadcast_to(
                lowered[:, s : s + 1], (rows, tokens)
            )

    projected, square_sum = own_partial, squares
    for copy in started:
        copy.wait_recv()
    for offset in range(1, lenders):
        projected = projected + q_recv[offset, :, :width]
        square_sum = square_sum + q_recv[offset, :, width : width + 1]
    inverse = lax.rsqrt(square_sum / (act_ref.shape[1] * lenders) + epsilon)
    normed = projected * inverse * head_dim ** (-0.5)
    q_all[me] = jnp.concatenate(
        [normed[:, j * head_dim : (j + 1) * head_dim] for j in range(chunk_heads)], axis=0
    ).astype(bf16)
    for offset in far_first:
        copy = to_lender(1, offset, q_all.at[me], q_all.at[me])
        copy.start()
        started.append(copy)

    step_slots = max(1, min(slot_count, 512 // tokens))
    step = step_slots * tokens
    steps = slot_count // step_slots
    eye = lax.broadcasted_iota(jnp.int32, (chunk_rows, LANES), 0) == lax.broadcasted_iota(
        jnp.int32, (chunk_rows, LANES), 1
    )
    first_line = lax.broadcasted_iota(jnp.int32, (SUBLANES, LANES), 0) == 0
    for h in range(kv_heads):
        chunks = range(h * chunks_per_kv, (h + 1) * chunks_per_kv)
        for source in chunks:

            @pl.when(me != source)
            def _():
                offset = lax.rem(me - source + lenders, lenders)
                to_lender(1, offset, q_all.at[source], q_all.at[source]).wait_recv()

        if h == 0:
            key_copy.wait()
        queries = q_all[chunks.start : chunks.stop].reshape(group * rows, head_dim)
        running = None
        for c in range(steps):
            block = keys[h, c * step_slots : (c + 1) * step_slots].reshape(step, head_dim)
            found = lax.dot_general(
                queries, block, (((1,), (1,)), ((), ())), preferred_element_type=f32
            )
            found = found.reshape(group, rows, step) + bias[h, :, c * step : (c + 1) * step][None]
            found = found.reshape(group * rows, step)
            scores[h, :, c * step : (c + 1) * step] = found
            for t in range(0, step, LANES):
                piece = found[:, t : t + LANES]
                running = piece if running is None else jnp.maximum(running, piece)
        best = jnp.max(running, axis=1, keepdims=True)
        if h == 0:
            value_copy.wait()
        total = None
        gathered = jnp.zeros((group * rows, head_dim), f32)
        for c in range(steps):
            weights = jnp.exp(scores[h, :, c * step : (c + 1) * step] - best)
            for t in range(0, step, LANES):
                piece = weights[:, t : t + LANES]
                total = piece if total is None else total + piece
            block = values[h, c * step_slots : (c + 1) * step_slots].reshape(step, head_dim)
            gathered = gathered + jnp.dot(
                weights.astype(bf16), block, preferred_element_type=f32
            )
        total = jnp.sum(total, axis=1, keepdims=True)
        for j, d in enumerate(chunks):
            lines = slice(j * chunk_rows, (j + 1) * chunk_rows)
            best_line = jnp.sum(jnp.where(eye, best[lines], 0.0), axis=0, keepdims=True)
            total_line = jnp.sum(jnp.where(eye, total[lines], 0.0), axis=0, keepdims=True)
            part_send[d, :chunk_rows, :] = gathered[lines]
            part_send[d, chunk_rows:, :] = jnp.where(first_line, best_line, total_line)
        for d in chunks:

            @pl.when(me != d)
            def _():
                offset = lax.rem(d - me + lenders, lenders)
                to_lender(2, offset, part_send.at[d], part_recv.at[offset]).start()

    part_recv[0] = part_send[me]
    for offset in range(1, lenders):
        copy = to_lender(2, offset, part_send.at[lender_at(offset)], part_recv.at[offset])
        copy.wait_recv()
        started.append(copy)
    bests, totals = [], []
    for offset in range(lenders):
        line = part_recv[offset, chunk_rows : chunk_rows + 1, :]
        bests.append(jnp.sum(jnp.where(eye, line, 0.0), axis=1, keepdims=True))
        line = part_recv[offset, chunk_rows + 1 : chunk_rows + 2, :]
        totals.append(jnp.sum(jnp.where(eye, line, 0.0), axis=1, keepdims=True))
    highest = functools.reduce(jnp.maximum, bests)
    home_total = jnp.zeros((chunk_rows, 1), f32)
    home_value = jnp.zeros((chunk_rows, head_dim), f32)
    for offset in range(lenders):
        factor = jnp.exp(bests[offset] - highest)
        home_total = home_total + totals[offset] * factor
        home_value = home_value + part_recv[offset, :chunk_rows, :] * factor
    att_all[me] = (home_value / home_total).astype(bf16)
    att_copies = {}
    for offset in far_first:
        copy = to_lender(3, offset, att_all.at[me], att_all.at[me])
        copy.start()
        att_copies[offset] = copy
    started += att_copies.values()

    product = None
    for offset in range(lenders):
        wo_copies[offset].wait()
        if offset > 0:
            att_copies[offset].wait_recv()
        chunk = att_all[lender_at(lenders - offset)].astype(f32)
        chunk = jnp.concatenate(
            [chunk[j * rows : (j + 1) * rows] for j in range(chunk_heads)], axis=1
        ).astype(bf16)
        term = jnp.dot(chunk, wo[offset], preferred_element_type=f32)
        product = term if product is None else product + term

    home_rows = rows // tensors
    part_width = product.shape[1] // tensors
    line_block = lax.broadcasted_iota(jnp.int32, (rows, part_width), 0) // home_rows
    for d in range(tensors):
        packed = jnp.zeros((rows, part_width), f32)
        for c in range(tensors):
            piece = product[:, c * part_width : (c + 1) * part_width]
            shift = (c - d) * home_rows % rows
            if shift:
                piece = pltpu.roll(piece, shift, 0)
            packed = jnp.where(line_block == c, piece, packed)
        sum_send[d] = packed
    for offset in range(1, tensors):
        target = lax.rem(mine + offset, tensors)
        copy = pltpu.make_async_remote_copy(
            src_ref=sum_send.at[target],
            dst_ref=sum_recv.at[offset],
            send_sem=tensor_send.at[offset],
            recv_sem=tensor_recv.at[offset],
            device_id={"tensor": target},
            device_id_type=MESH,
        )
        copy.start()
        started.append(copy)
    result = sum_send[mine]
    for copy in started[1 - tensors :] if tensors > 1 else []:
        copy.wait_recv()
    for offset in range(1, tensors):
        result = result + sum_recv[offset]
    for c in range(tensors):
        out_ref[:, c * part_width : (c + 1) * part_width] = result[
            c * home_rows : (c + 1) * home_rows
        ].astype(out_ref.dtype)
    for copy in started:
        copy.wait_send()


def fused(
    activations,
    norm_gain,
    w_query,
    w_out,
    key_pool,
    value_block_store,
    block_list,
    block_slot_table,
    kept_len,
):
    lenders, tensors = lax.axis_size("lender"), lax.axis_size("tensor")
    rows, depth = activations.shape
    kv_heads, slot_count, tokens, head_dim = key_pool.shape
    width = w_query.shape[1] // lenders
    out_width = w_out.shape[1]
    chunk_rows = width // head_dim * rows
    group_rows = w_query.shape[1] // head_dim // kv_heads * rows
    part_width = out_width // tensors
    f32, bf16 = jnp.float32, jnp.bfloat16
    vmem = pl.BlockSpec(memory_space=pltpu.VMEM)
    hbm = pl.BlockSpec(memory_space=pltpu.HBM)
    return pl.pallas_call(
        functools.partial(fused_kernel, lenders, tensors),
        out_shape=jax.ShapeDtypeStruct((rows // tensors, out_width), bf16),
        in_specs=[hbm] * 9,
        out_specs=vmem,
        scratch_shapes=[
            pltpu.VMEM(activations.shape, bf16),
            pltpu.VMEM(norm_gain.shape, bf16),
            pltpu.VMEM(block_list.shape, jnp.int32),
            pltpu.VMEM(block_slot_table.shape, jnp.int32),
            pltpu.VMEM(kept_len.shape[::-1], jnp.int32),
            pltpu.VMEM((lenders, depth, width), bf16),
            pltpu.VMEM((lenders, width, out_width), bf16),
            pltpu.VMEM(key_pool.shape, bf16),
            pltpu.VMEM(key_pool.shape, bf16),
            pltpu.VMEM((lenders, rows, width + LANES), f32),
            pltpu.VMEM((lenders, rows, width + LANES), f32),
            pltpu.VMEM((lenders, chunk_rows, head_dim), bf16),
            pltpu.VMEM((kv_heads, rows, slot_count * tokens), f32),
            pltpu.VMEM((kv_heads, group_rows, slot_count * tokens), f32),
            pltpu.VMEM((lenders, chunk_rows + SUBLANES, head_dim), f32),
            pltpu.VMEM((lenders, chunk_rows + SUBLANES, head_dim), f32),
            pltpu.VMEM((lenders, chunk_rows, head_dim), bf16),
            pltpu.VMEM((tensors, rows, part_width), f32),
            pltpu.VMEM((tensors, rows, part_width), f32),
            pltpu.SemaphoreType.DMA((5,)),
            pltpu.SemaphoreType.DMA((lenders,)),
            pltpu.SemaphoreType.DMA((lenders,)),
            pltpu.SemaphoreType.DMA((2,)),
            pltpu.SemaphoreType.DMA((4, lenders)),
            pltpu.SemaphoreType.DMA((4, lenders)),
            pltpu.SemaphoreType.DMA((tensors,)),
            pltpu.SemaphoreType.DMA((tensors,)),
        ],
        compiler_params=pltpu.CompilerParams(
            collective_id=0, has_side_effects=True, vmem_limit_bytes=64 * 2**20
        ),
        name="decode_attention",
    )(
        activations,
        norm_gain,
        block_list,
        block_slot_table,
        kept_len.T,
        w_query,
        w_out,
        key_pool,
        value_block_store,
    )


def per_device(*arrays):
    activations, _, w_query, w_out, key_pool = arrays[:5]
    lenders, tensors = lax.axis_size("lender"), lax.axis_size("tensor")
    rows = activations.shape[0]
    kv_heads, slot_count, tokens, head_dim = key_pool.shape
    columns, out_width = w_query.shape[1], w_out.shape[1]
    width = columns // lenders
    fits = (
        rows == SUBLANES
        and head_dim == LANES
        and tokens == LANES
        and columns % (lenders * head_dim) == 0
        and columns // kv_heads % max(width, 1) == 0
        and width * rows % (2 * SUBLANES * head_dim) == 0
        and width * rows <= LANES * head_dim
        and rows % tensors == 0
        and out_width % (tensors * LANES) == 0
        and slot_count * tokens % 512 == 0
    )
    return (fused if fits else separate_ops)(*arrays)


def solution(mesh):
    in_specs = (
        P("group", "lender"),
        P("lender"),
        P("lender", "tensor"),
        P("tensor", "lender"),
        P("tensor", ("group", "lender"), None, None),
        P("tensor", ("group", "lender"), None, None),
        P("group", "tensor", None),
        P("tensor", "group"),
        P("group", "tensor"),
    )
    out_specs = P(("group", "tensor"), "lender")
    return jax.shard_map(
        per_device, mesh=mesh, in_specs=in_specs, out_specs=out_specs, check_vma=False
    )
```

```python
import functools

import jax
import jax.numpy as jnp
from jax import lax
from jax.experimental import pallas as pl
from jax.experimental.pallas import tpu as pltpu
from jax.sharding import PartitionSpec as P

very_low = -1e30
epsilon = 1e-05


def separate_ops(
    activations,
    norm_gain,
    w_query,
    w_out,
    key_pool,
    value_block_store,
    block_list,
    block_slot_table,
    kept_len,
):
    row_count = activations.shape[0]
    kv_heads = key_pool.shape[0]
    slot_count = key_pool.shape[1]
    head_dim = key_pool.shape[3]
    kept_most = block_list.shape[2]
    features = activations.astype(jnp.float32)
    squares = jnp.sum(features * features, axis=1)
    scaled = (features * norm_gain.astype(jnp.float32)).astype(jnp.bfloat16)
    partial_value = jnp.dot(scaled, w_query, preferred_element_type=jnp.float32)
    projected, square_sum = lax.psum((partial_value, squares), "lender")
    width = features.shape[1] * lax.axis_size("lender")
    inverse = lax.rsqrt(square_sum / width + epsilon)
    query_vectors = (projected * inverse[:, None] * head_dim ** (-0.5)).astype(jnp.bfloat16)
    group_size = query_vectors.shape[1] // (kv_heads * head_dim)
    query_vectors = query_vectors.reshape(row_count, kv_heads, group_size, head_dim)
    slot_lookup_table = jnp.broadcast_to(
        block_slot_table[None], (row_count,) + block_slot_table.shape
    )
    slot_ids = jnp.take_along_axis(slot_lookup_table, block_list, axis=2)
    positions = jnp.arange(kept_most, dtype=jnp.int32)
    is_live = positions[None, None, :] < kept_len[:, :, None]
    local_slot = slot_ids - lax.axis_index("lender") * slot_count
    matches = is_live[..., None] & (
        local_slot[..., None] == jnp.arange(slot_count, dtype=jnp.int32)
    )
    owner_mask = jnp.transpose(jnp.any(matches, axis=2), (1, 2, 0))
    owner_half = owner_mask.astype(jnp.bfloat16)
    owner_full = owner_mask.astype(jnp.float32)
    used_slot = jnp.any(owner_mask, axis=2)
    picked = jnp.einsum(
        "hsr,rhgd->hsgd", owner_half, query_vectors, preferred_element_type=jnp.float32
    ).astype(jnp.bfloat16)
    scores = jnp.einsum("hsgd,hstd->hsgt", picked, key_pool, preferred_element_type=jnp.float32)
    block_best = jnp.max(scores, axis=3)
    spread = jnp.where(owner_mask[..., None], block_best[:, :, None, :], very_low)
    row_best = jnp.max(spread, axis=1)
    slot_best = jnp.max(jnp.where(owner_mask[..., None], row_best[:, None, :, :], very_low), axis=2)
    slot_best = jnp.where(used_slot[..., None], slot_best, 0.0)
    weights_full = jnp.where(
        used_slot[:, :, None, None], jnp.exp(scores - slot_best[..., None]), 0.0
    )
    slot_weight = jnp.sum(weights_full, axis=3)
    slot_value = jnp.einsum(
        "hsgt,hstd->hsgd",
        weights_full.astype(jnp.bfloat16),
        value_block_store,
        preferred_element_type=jnp.float32,
    )
    row_weight = jnp.einsum(
        "hsr,hsg->rhg", owner_full, slot_weight, precision=lax.Precision.HIGHEST
    )
    row_value = jnp.einsum(
        "hsr,hsgd->rhgd", owner_full, slot_value, precision=lax.Precision.HIGHEST
    )
    row_high = jnp.transpose(row_best, (1, 0, 2))
    lenders = lax.axis_size("lender")
    home_rows = row_count // lenders
    came_best, came_weight, came_value = (
        lax.all_to_all(row_high, "lender", split_axis=0, concat_axis=0, tiled=True),
        lax.all_to_all(row_weight, "lender", split_axis=0, concat_axis=0, tiled=True),
        lax.all_to_all(row_value, "lender", split_axis=0, concat_axis=0, tiled=True),
    )
    came_best = came_best.reshape((lenders, home_rows) + came_best.shape[1:])
    came_weight = came_weight.reshape((lenders, home_rows) + came_weight.shape[1:])
    came_value = came_value.reshape((lenders, home_rows) + came_value.shape[1:])
    highest = jnp.max(came_best, axis=0)
    factor = jnp.exp(came_best - highest[None])
    home_weight = jnp.sum(came_weight * factor, axis=0)
    home_value = jnp.sum(came_value * factor[..., None], axis=0)
    home_attended = (
        (home_value / home_weight[..., None]).astype(jnp.bfloat16).reshape(home_rows, -1)
    )
    attended = lax.all_gather(home_attended, "lender", axis=0, tiled=True)
    result = lax.psum_scatter(
        jnp.dot(attended, w_out, preferred_element_type=jnp.float32),
        "tensor",
        scatter_dimension=0,
        tiled=True,
    )
    return result.astype(jnp.bfloat16)


MESH = pl.DeviceIdType.MESH
LANES = 128
SUBLANES = 8


def fused_kernel(
    lenders,
    tensors,
    act_hbm,
    gain_hbm,
    list_hbm,
    table_hbm,
    kept_hbm,
    wq_hbm,
    wo_hbm,
    key_hbm,
    value_hbm,
    out_ref,
    act_ref,
    gain_ref,
    list_ref,
    table_ref,
    kept_ref,
    wq,
    wo,
    keys,
    values,
    q_send,
    q_recv,
    q_all,
    bias,
    scores,
    part_send,
    part_recv,
    att_all,
    sum_send,
    sum_recv,
    small_sem,
    wq_sem,
    wo_sem,
    kv_sem,
    lender_send,
    lender_recv,
    tensor_send,
    tensor_recv,
):
    me = lax.axis_index("lender")
    mine = lax.axis_index("tensor")
    rows = act_ref.shape[0]
    kv_heads, slot_count, tokens, head_dim = keys.shape
    width = wq.shape[2]
    chunk_heads = width // head_dim
    chunk_rows = chunk_heads * rows
    group = wo.shape[0] * chunk_heads // kv_heads
    chunks_per_kv = group // chunk_heads
    kept_most = list_ref.shape[2]
    f32, bf16 = jnp.float32, jnp.bfloat16

    def lender_at(offset):
        return lax.rem(me + offset, lenders)

    far_first = sorted(range(1, lenders), key=lambda offset: abs(2 * offset - lenders))
    small_copies = [
        pltpu.make_async_copy(src, dst, small_sem.at[at])
        for at, (src, dst) in enumerate(
            (
                (act_hbm, act_ref),
                (gain_hbm, gain_ref),
                (list_hbm, list_ref),
                (table_hbm, table_ref),
                (kept_hbm, kept_ref),
            )
        )
    ]
    wq_copies = []
    for offset in far_first + [0]:
        columns = pl.ds(pl.multiple_of(lender_at(offset) * width, width), width)
        wq_copies.append(
            pltpu.make_async_copy(wq_hbm.at[:, columns], wq.at[offset], wq_sem.at[offset])
        )
    key_copy = pltpu.make_async_copy(key_hbm, keys, kv_sem.at[0])
    value_copy = pltpu.make_async_copy(value_hbm, values, kv_sem.at[1])
    wo_copies = []
    for offset in range(lenders):
        source = lender_at(lenders - offset)
        lines = pl.ds(pl.multiple_of(source * width, width), width)
        wo_copies.append(
            pltpu.make_async_copy(wo_hbm.at[lines], wo.at[offset], wo_sem.at[offset])
        )
    for copy in small_copies[:2]:
        copy.start()
    for copy in wq_copies:
        copy.start()

    barrier = pltpu.get_barrier_semaphore()
    for offset in range(1, lenders):
        pl.semaphore_signal(
            barrier, inc=1, device_id={"lender": lender_at(offset)}, device_id_type=MESH
        )
    for offset in range(1, tensors):
        pl.semaphore_signal(
            barrier,
            inc=1,
            device_id={"tensor": lax.rem(mine + offset, tensors)},
            device_id_type=MESH,
        )

    def to_lender(stage, offset, src, dst):
        return pltpu.make_async_remote_copy(
            src_ref=src,
            dst_ref=dst,
            send_sem=lender_send.at[stage, offset],
            recv_sem=lender_recv.at[stage, offset],
            device_id={"lender": lender_at(offset)},
            device_id_type=MESH,
        )

    for copy in small_copies[:2]:
        copy.wait()
    features = act_ref[...].astype(f32)
    squares = jnp.sum(features * features, axis=1, keepdims=True)
    scaled = (features * gain_ref[...].astype(f32).reshape(1, -1)).astype(bf16)

    started = []
    own_partial = None
    for at, offset in enumerate(far_first + [0]):
        wq_copies[at].wait()
        if at == 0:
            for copy in small_copies[2:]:
                copy.start()
            key_copy.start()
            value_copy.start()
        if at == min(1, lenders - 1):
            for copy in wo_copies:
                copy.start()
        partial = jnp.dot(scaled, wq[offset], preferred_element_type=f32)
        if offset == 0:
            own_partial = partial
            continue
        q_send[offset, :, :width] = partial
        q_send[offset, :, width:] = jnp.broadcast_to(squares, (rows, LANES))
        if at == 0:
            pl.semaphore_wait(barrier, lenders + tensors - 2)
        copy = to_lender(0, offset, q_send.at[offset], q_recv.at[offset])
        copy.start()
        started.append(copy)

    for copy in small_copies[2:]:
        copy.wait()
    blocks = table_ref.shape[1]
    block_ids = lax.broadcasted_iota(jnp.int32, (rows, blocks), 1)
    local_slots = lax.broadcasted_iota(jnp.int32, (slot_count, blocks), 0) + me * slot_count
    row_eye = lax.broadcasted_iota(jnp.int32, (rows, rows), 0) == lax.broadcasted_iota(
        jnp.int32, (rows, rows), 1
    )
    for h in range(kv_heads):
        member = jnp.zeros((rows, blocks), f32)
        listed = list_ref[:, h, :]
        kept = jnp.sum(jnp.where(row_eye, kept_ref[h : h + 1, :], 0), axis=1, keepdims=True)
        for k in range(kept_most):
            hit = (listed[:, k : k + 1] == block_ids) & (kept > k)
            member = jnp.where(hit, 1.0, member)
        holds = jnp.where(table_ref[h : h + 1, :] == local_slots, 1.0, 0.0)
        owner = lax.dot_general(
            member.astype(bf16),
            holds.astype(bf16),
            (((1,), (1,)), ((), ())),
            preferred_element_type=f32,
        )
        lowered = (owner - 1.0) * -very_low
        for s in range(slot_count):
            bias[h, :, s * tokens : (s + 1) * tokens] = jnp.broadcast_to(
                lowered[:, s : s + 1], (rows, tokens)
            )

    projected, square_sum = own_partial, squares
    for copy in started:
        copy.wait_recv()
    for offset in range(1, lenders):
        projected = projected + q_recv[offset, :, :width]
        square_sum = square_sum + q_recv[offset, :, width : width + 1]
    inverse = lax.rsqrt(square_sum / (act_ref.shape[1] * lenders) + epsilon)
    normed = projected * inverse * head_dim ** (-0.5)
    q_all[me] = jnp.concatenate(
        [normed[:, j * head_dim : (j + 1) * head_dim] for j in range(chunk_heads)], axis=0
    ).astype(bf16)
    for offset in far_first:
        copy = to_lender(1, offset, q_all.at[me], q_all.at[me])
        copy.start()
        started.append(copy)

    step_slots = max(1, min(slot_count, 512 // tokens))
    step = step_slots * tokens
    steps = slot_count // step_slots
    eye = lax.broadcasted_iota(jnp.int32, (chunk_rows, LANES), 0) == lax.broadcasted_iota(
        jnp.int32, (chunk_rows, LANES), 1
    )
    first_line = lax.broadcasted_iota(jnp.int32, (SUBLANES, LANES), 0) == 0
    for h in range(kv_heads):
        chunks = range(h * chunks_per_kv, (h + 1) * chunks_per_kv)
        for source in chunks:

            @pl.when(me != source)
            def _():
                offset = lax.rem(me - source + lenders, lenders)
                to_lender(1, offset, q_all.at[source], q_all.at[source]).wait_recv()

        if h == 0:
            key_copy.wait()
        queries = q_all[chunks.start : chunks.stop].reshape(group * rows, head_dim)
        running = None
        for c in range(steps):
            block = keys[h, c * step_slots : (c + 1) * step_slots].reshape(step, head_dim)
            found = lax.dot_general(
                queries, block, (((1,), (1,)), ((), ())), preferred_element_type=f32
            )
            found = found.reshape(group, rows, step) + bias[h, :, c * step : (c + 1) * step][None]
            found = found.reshape(group * rows, step)
            scores[h, :, c * step : (c + 1) * step] = found
            for t in range(0, step, LANES):
                piece = found[:, t : t + LANES]
                running = piece if running is None else jnp.maximum(running, piece)
        best = jnp.max(running, axis=1, keepdims=True)
        if h == 0:
            value_copy.wait()
        total = None
        gathered = jnp.zeros((group * rows, head_dim), f32)
        for c in range(steps):
            weights = jnp.exp(scores[h, :, c * step : (c + 1) * step] - best)
            for t in range(0, step, LANES):
                piece = weights[:, t : t + LANES]
                total = piece if total is None else total + piece
            block = values[h, c * step_slots : (c + 1) * step_slots].reshape(step, head_dim)
            gathered = gathered + jnp.dot(
                weights.astype(bf16), block, preferred_element_type=f32
            )
        total = jnp.sum(total, axis=1, keepdims=True)
        for j, d in enumerate(chunks):
            lines = slice(j * chunk_rows, (j + 1) * chunk_rows)
            best_line = jnp.sum(jnp.where(eye, best[lines], 0.0), axis=0, keepdims=True)
            total_line = jnp.sum(jnp.where(eye, total[lines], 0.0), axis=0, keepdims=True)
            part_send[d, :chunk_rows, :] = gathered[lines]
            part_send[d, chunk_rows:, :] = jnp.where(first_line, best_line, total_line)
        for d in chunks:

            @pl.when(me != d)
            def _():
                offset = lax.rem(d - me + lenders, lenders)
                to_lender(2, offset, part_send.at[d], part_recv.at[offset]).start()

    part_recv[0] = part_send[me]
    for offset in range(1, lenders):
        copy = to_lender(2, offset, part_send.at[lender_at(offset)], part_recv.at[offset])
        copy.wait_recv()
        started.append(copy)
    bests, totals = [], []
    for offset in range(lenders):
        line = part_recv[offset, chunk_rows : chunk_rows + 1, :]
        bests.append(jnp.sum(jnp.where(eye, line, 0.0), axis=1, keepdims=True))
        line = part_recv[offset, chunk_rows + 1 : chunk_rows + 2, :]
        totals.append(jnp.sum(jnp.where(eye, line, 0.0), axis=1, keepdims=True))
    highest = functools.reduce(jnp.maximum, bests)
    home_total = jnp.zeros((chunk_rows, 1), f32)
    home_value = jnp.zeros((chunk_rows, head_dim), f32)
    for offset in range(lenders):
        factor = jnp.exp(bests[offset] - highest)
        home_total = home_total + totals[offset] * factor
        home_value = home_value + part_recv[offset, :chunk_rows, :] * factor
    att_all[me] = (home_value / home_total).astype(bf16)
    att_copies = {}
    for offset in far_first:
        copy = to_lender(3, offset, att_all.at[me], att_all.at[me])
        copy.start()
        att_copies[offset] = copy
    started += att_copies.values()

    product = None
    for offset in range(lenders):
        wo_copies[offset].wait()
        if offset > 0:
            att_copies[offset].wait_recv()
        chunk = att_all[lender_at(lenders - offset)].astype(f32)
        chunk = jnp.concatenate(
            [chunk[j * rows : (j + 1) * rows] for j in range(chunk_heads)], axis=1
        ).astype(bf16)
        term = jnp.dot(chunk, wo[offset], preferred_element_type=f32)
        product = term if product is None else product + term

    home_rows = rows // tensors
    part_width = product.shape[1] // tensors
    line_block = lax.broadcasted_iota(jnp.int32, (rows, part_width), 0) // home_rows
    for d in range(tensors):
        packed = jnp.zeros((rows, part_width), f32)
        for c in range(tensors):
            piece = product[:, c * part_width : (c + 1) * part_width]
            shift = (c - d) * home_rows % rows
            if shift:
                piece = pltpu.roll(piece, shift, 0)
            packed = jnp.where(line_block == c, piece, packed)
        sum_send[d] = packed
    for offset in range(1, tensors):
        target = lax.rem(mine + offset, tensors)
        copy = pltpu.make_async_remote_copy(
            src_ref=sum_send.at[target],
            dst_ref=sum_recv.at[offset],
            send_sem=tensor_send.at[offset],
            recv_sem=tensor_recv.at[offset],
            device_id={"tensor": target},
            device_id_type=MESH,
        )
        copy.start()
        started.append(copy)
    result = sum_send[mine]
    for copy in started[1 - tensors :] if tensors > 1 else []:
        copy.wait_recv()
    for offset in range(1, tensors):
        result = result + sum_recv[offset]
    for c in range(tensors):
        out_ref[:, c * part_width : (c + 1) * part_width] = result[
            c * home_rows : (c + 1) * home_rows
        ].astype(out_ref.dtype)
    for copy in started:
        copy.wait_send()


def fused(
    activations,
    norm_gain,
    w_query,
    w_out,
    key_pool,
    value_block_store,
    block_list,
    block_slot_table,
    kept_len,
):
    lenders, tensors = lax.axis_size("lender"), lax.axis_size("tensor")
    rows, depth = activations.shape
    kv_heads, slot_count, tokens, head_dim = key_pool.shape
    width = w_query.shape[1] // lenders
    out_width = w_out.shape[1]
    chunk_rows = width // head_dim * rows
    group_rows = w_query.shape[1] // head_dim // kv_heads * rows
    part_width = out_width // tensors
    f32, bf16 = jnp.float32, jnp.bfloat16
    vmem = pl.BlockSpec(memory_space=pltpu.VMEM)
    hbm = pl.BlockSpec(memory_space=pltpu.HBM)
    return pl.pallas_call(
        functools.partial(fused_kernel, lenders, tensors),
        out_shape=jax.ShapeDtypeStruct((rows // tensors, out_width), bf16),
        in_specs=[hbm] * 9,
        out_specs=vmem,
        scratch_shapes=[
            pltpu.VMEM(activations.shape, bf16),
            pltpu.VMEM(norm_gain.shape, bf16),
            pltpu.VMEM(block_list.shape, jnp.int32),
            pltpu.VMEM(block_slot_table.shape, jnp.int32),
            pltpu.VMEM(kept_len.shape[::-1], jnp.int32),
            pltpu.VMEM((lenders, depth, width), bf16),
            pltpu.VMEM((lenders, width, out_width), bf16),
            pltpu.VMEM(key_pool.shape, bf16),
            pltpu.VMEM(key_pool.shape, bf16),
            pltpu.VMEM((lenders, rows, width + LANES), f32),
            pltpu.VMEM((lenders, rows, width + LANES), f32),
            pltpu.VMEM((lenders, chunk_rows, head_dim), bf16),
            pltpu.VMEM((kv_heads, rows, slot_count * tokens), f32),
            pltpu.VMEM((kv_heads, group_rows, slot_count * tokens), f32),
            pltpu.VMEM((lenders, chunk_rows + SUBLANES, head_dim), f32),
            pltpu.VMEM((lenders, chunk_rows + SUBLANES, head_dim), f32),
            pltpu.VMEM((lenders, chunk_rows, head_dim), bf16),
            pltpu.VMEM((tensors, rows, part_width), f32),
            pltpu.VMEM((tensors, rows, part_width), f32),
            pltpu.SemaphoreType.DMA((5,)),
            pltpu.SemaphoreType.DMA((lenders,)),
            pltpu.SemaphoreType.DMA((lenders,)),
            pltpu.SemaphoreType.DMA((2,)),
            pltpu.SemaphoreType.DMA((4, lenders)),
            pltpu.SemaphoreType.DMA((4, lenders)),
            pltpu.SemaphoreType.DMA((tensors,)),
            pltpu.SemaphoreType.DMA((tensors,)),
        ],
        compiler_params=pltpu.CompilerParams(
            collective_id=0, has_side_effects=True, vmem_limit_bytes=48 * 2**20
        ),
        name="decode_attention",
    )(
        *(
            pltpu.with_memory_space_constraint(array, pltpu.HBM)
            for array in (
                activations,
                norm_gain,
                block_list,
                block_slot_table,
                kept_len.T,
                w_query,
                w_out,
                key_pool,
                value_block_store,
            )
        )
    )


def per_device(*arrays):
    activations, _, w_query, w_out, key_pool = arrays[:5]
    lenders, tensors = lax.axis_size("lender"), lax.axis_size("tensor")
    rows = activations.shape[0]
    kv_heads, slot_count, tokens, head_dim = key_pool.shape
    columns, out_width = w_query.shape[1], w_out.shape[1]
    width = columns // lenders
    fits = (
        rows == SUBLANES
        and head_dim == LANES
        and tokens == LANES
        and columns % (lenders * head_dim) == 0
        and columns // kv_heads % max(width, 1) == 0
        and width * rows % (2 * SUBLANES * head_dim) == 0
        and width * rows <= LANES * head_dim
        and rows % tensors == 0
        and out_width % (tensors * LANES) == 0
        and slot_count * tokens % 512 == 0
    )
    return (fused if fits else separate_ops)(*arrays)


def solution(mesh):
    in_specs = (
        P("group", "lender"),
        P("lender"),
        P("lender", "tensor"),
        P("tensor", "lender"),
        P("tensor", ("group", "lender"), None, None),
        P("tensor", ("group", "lender"), None, None),
        P("group", "tensor", None),
        P("tensor", "group"),
        P("group", "tensor"),
    )
    out_specs = P(("group", "tensor"), "lender")
    return jax.shard_map(
        per_device, mesh=mesh, in_specs=in_specs, out_specs=out_specs, check_vma=False
    )
```

```python
import functools

import jax
import jax.numpy as jnp
from jax import lax
from jax.experimental import pallas as pl
from jax.experimental.pallas import tpu as pltpu
from jax.sharding import PartitionSpec as P

very_low = -1e30
epsilon = 1e-05


def separate_ops(
    activations,
    norm_gain,
    w_query,
    w_out,
    key_pool,
    value_block_store,
    block_list,
    block_slot_table,
    kept_len,
):
    row_count = activations.shape[0]
    kv_heads = key_pool.shape[0]
    slot_count = key_pool.shape[1]
    head_dim = key_pool.shape[3]
    kept_most = block_list.shape[2]
    features = activations.astype(jnp.float32)
    squares = jnp.sum(features * features, axis=1)
    scaled = (features * norm_gain.astype(jnp.float32)).astype(jnp.bfloat16)
    partial_value = jnp.dot(scaled, w_query, preferred_element_type=jnp.float32)
    projected, square_sum = lax.psum((partial_value, squares), "lender")
    width = features.shape[1] * lax.axis_size("lender")
    inverse = lax.rsqrt(square_sum / width + epsilon)
    query_vectors = (projected * inverse[:, None] * head_dim ** (-0.5)).astype(jnp.bfloat16)
    group_size = query_vectors.shape[1] // (kv_heads * head_dim)
    query_vectors = query_vectors.reshape(row_count, kv_heads, group_size, head_dim)
    slot_lookup_table = jnp.broadcast_to(
        block_slot_table[None], (row_count,) + block_slot_table.shape
    )
    slot_ids = jnp.take_along_axis(slot_lookup_table, block_list, axis=2)
    positions = jnp.arange(kept_most, dtype=jnp.int32)
    is_live = positions[None, None, :] < kept_len[:, :, None]
    local_slot = slot_ids - lax.axis_index("lender") * slot_count
    matches = is_live[..., None] & (
        local_slot[..., None] == jnp.arange(slot_count, dtype=jnp.int32)
    )
    owner_mask = jnp.transpose(jnp.any(matches, axis=2), (1, 2, 0))
    owner_half = owner_mask.astype(jnp.bfloat16)
    owner_full = owner_mask.astype(jnp.float32)
    used_slot = jnp.any(owner_mask, axis=2)
    picked = jnp.einsum(
        "hsr,rhgd->hsgd", owner_half, query_vectors, preferred_element_type=jnp.float32
    ).astype(jnp.bfloat16)
    scores = jnp.einsum("hsgd,hstd->hsgt", picked, key_pool, preferred_element_type=jnp.float32)
    block_best = jnp.max(scores, axis=3)
    spread = jnp.where(owner_mask[..., None], block_best[:, :, None, :], very_low)
    row_best = jnp.max(spread, axis=1)
    slot_best = jnp.max(jnp.where(owner_mask[..., None], row_best[:, None, :, :], very_low), axis=2)
    slot_best = jnp.where(used_slot[..., None], slot_best, 0.0)
    weights_full = jnp.where(
        used_slot[:, :, None, None], jnp.exp(scores - slot_best[..., None]), 0.0
    )
    slot_weight = jnp.sum(weights_full, axis=3)
    slot_value = jnp.einsum(
        "hsgt,hstd->hsgd",
        weights_full.astype(jnp.bfloat16),
        value_block_store,
        preferred_element_type=jnp.float32,
    )
    row_weight = jnp.einsum(
        "hsr,hsg->rhg", owner_full, slot_weight, precision=lax.Precision.HIGHEST
    )
    row_value = jnp.einsum(
        "hsr,hsgd->rhgd", owner_full, slot_value, precision=lax.Precision.HIGHEST
    )
    row_high = jnp.transpose(row_best, (1, 0, 2))
    lenders = lax.axis_size("lender")
    home_rows = row_count // lenders
    came_best, came_weight, came_value = (
        lax.all_to_all(row_high, "lender", split_axis=0, concat_axis=0, tiled=True),
        lax.all_to_all(row_weight, "lender", split_axis=0, concat_axis=0, tiled=True),
        lax.all_to_all(row_value, "lender", split_axis=0, concat_axis=0, tiled=True),
    )
    came_best = came_best.reshape((lenders, home_rows) + came_best.shape[1:])
    came_weight = came_weight.reshape((lenders, home_rows) + came_weight.shape[1:])
    came_value = came_value.reshape((lenders, home_rows) + came_value.shape[1:])
    highest = jnp.max(came_best, axis=0)
    factor = jnp.exp(came_best - highest[None])
    home_weight = jnp.sum(came_weight * factor, axis=0)
    home_value = jnp.sum(came_value * factor[..., None], axis=0)
    home_attended = (
        (home_value / home_weight[..., None]).astype(jnp.bfloat16).reshape(home_rows, -1)
    )
    attended = lax.all_gather(home_attended, "lender", axis=0, tiled=True)
    result = lax.psum_scatter(
        jnp.dot(attended, w_out, preferred_element_type=jnp.float32),
        "tensor",
        scatter_dimension=0,
        tiled=True,
    )
    return result.astype(jnp.bfloat16)


MESH = pl.DeviceIdType.MESH
LANES = 128
SUBLANES = 8


def fused_kernel(
    groups,
    lenders,
    tensors,
    act_hbm,
    gain_hbm,
    list_hbm,
    table_hbm,
    kept_hbm,
    wq_hbm,
    wo_hbm,
    key_hbm,
    value_hbm,
    out_ref,
    act_ref,
    gain_ref,
    list_ref,
    table_ref,
    kept_ref,
    wq,
    wo,
    keys,
    values,
    q_send,
    q_recv,
    q_all,
    bias,
    scores,
    part_send,
    part_recv,
    att_all,
    sum_send,
    sum_recv,
    small_sem,
    wq_sem,
    wo_sem,
    kv_sem,
    lender_send,
    lender_recv,
    att_send,
    att_recv,
    tensor_send,
    tensor_recv,
):
    part = lax.axis_index("group")
    me = lax.axis_index("lender")
    mine = lax.axis_index("tensor")
    rows = act_ref.shape[0]
    kv_heads, slot_count, tokens, head_dim = keys.shape
    width = wq.shape[2]
    chunk_heads = width // head_dim
    chunk_rows = chunk_heads * rows
    group = wo.shape[0] * chunk_heads // kv_heads
    share = wo.shape[2]
    chunks_per_kv = group // chunk_heads
    kept_most = list_ref.shape[2]
    f32, bf16 = jnp.float32, jnp.bfloat16

    def lender_at(offset):
        return lax.rem(me + offset, lenders)

    far_first = sorted(range(1, lenders), key=lambda offset: abs(2 * offset - lenders))
    small_copies = [
        pltpu.make_async_copy(src, dst, small_sem.at[at])
        for at, (src, dst) in enumerate(
            (
                (act_hbm, act_ref),
                (gain_hbm, gain_ref),
                (list_hbm, list_ref),
                (table_hbm, table_ref),
                (kept_hbm, kept_ref),
            )
        )
    ]
    wq_copies = []
    for offset in far_first + [0]:
        columns = pl.ds(pl.multiple_of(lender_at(offset) * width, width), width)
        wq_copies.append(
            pltpu.make_async_copy(wq_hbm.at[:, columns], wq.at[offset], wq_sem.at[offset])
        )
    key_copy = pltpu.make_async_copy(key_hbm, keys, kv_sem.at[0])
    value_copy = pltpu.make_async_copy(value_hbm, values, kv_sem.at[1])
    wo_copies = []
    for offset in range(lenders):
        source = lender_at(lenders - offset)
        lines = pl.ds(pl.multiple_of(source * width, width), width)
        columns = pl.ds(pl.multiple_of(part * share, share), share)
        wo_copies.append(
            pltpu.make_async_copy(wo_hbm.at[lines, columns], wo.at[offset], wo_sem.at[offset])
        )
    for copy in small_copies[:2]:
        copy.start()
    for copy in wq_copies:
        copy.start()

    barrier = pltpu.get_barrier_semaphore()
    def group_at(step):
        return lax.rem(part + step, groups)

    def tensor_at(offset):
        return lax.rem(mine + offset, tensors)

    greeted = [
        {"group": group_at(step), "lender": lender_at(offset)}
        for step in range(groups)
        for offset in range(lenders)
        if (step, offset) != (0, 0)
    ] + [
        {"group": group_at(step), "tensor": tensor_at(offset)}
        for step in range(groups)
        for offset in range(1, tensors)
    ]
    for device in greeted:
        pl.semaphore_signal(barrier, inc=1, device_id=device, device_id_type=MESH)

    def to_lender(stage, offset, src, dst):
        return pltpu.make_async_remote_copy(
            src_ref=src,
            dst_ref=dst,
            send_sem=lender_send.at[stage, offset],
            recv_sem=lender_recv.at[stage, offset],
            device_id={"lender": lender_at(offset)},
            device_id_type=MESH,
        )

    for copy in small_copies[:2]:
        copy.wait()
    features = act_ref[...].astype(f32)
    squares = jnp.sum(features * features, axis=1, keepdims=True)
    scaled = (features * gain_ref[...].astype(f32).reshape(1, -1)).astype(bf16)

    started = []
    own_partial = None
    for at, offset in enumerate(far_first + [0]):
        wq_copies[at].wait()
        if at == 0:
            for copy in small_copies[2:]:
                copy.start()
            key_copy.start()
            value_copy.start()
        if at == min(1, lenders - 1):
            for copy in wo_copies:
                copy.start()
        partial = jnp.dot(scaled, wq[offset], preferred_element_type=f32)
        if offset == 0:
            own_partial = partial
            continue
        q_send[offset, :, :width] = partial
        q_send[offset, :, width:] = jnp.broadcast_to(squares, (rows, LANES))
        if at == 0:
            pl.semaphore_wait(barrier, len(greeted))
        copy = to_lender(0, offset, q_send.at[offset], q_recv.at[offset])
        copy.start()
        started.append(copy)

    for copy in small_copies[2:]:
        copy.wait()
    blocks = table_ref.shape[1]
    block_ids = lax.broadcasted_iota(jnp.int32, (rows, blocks), 1)
    local_slots = lax.broadcasted_iota(jnp.int32, (slot_count, blocks), 0) + me * slot_count
    row_eye = lax.broadcasted_iota(jnp.int32, (rows, rows), 0) == lax.broadcasted_iota(
        jnp.int32, (rows, rows), 1
    )
    for h in range(kv_heads):
        member = jnp.zeros((rows, blocks), f32)
        listed = list_ref[:, h, :]
        kept = jnp.sum(jnp.where(row_eye, kept_ref[h : h + 1, :], 0), axis=1, keepdims=True)
        for k in range(kept_most):
            hit = (listed[:, k : k + 1] == block_ids) & (kept > k)
            member = jnp.where(hit, 1.0, member)
        holds = jnp.where(table_ref[h : h + 1, :] == local_slots, 1.0, 0.0)
        owner = lax.dot_general(
            member.astype(bf16),
            holds.astype(bf16),
            (((1,), (1,)), ((), ())),
            preferred_element_type=f32,
        )
        lowered = (owner - 1.0) * -very_low
        for s in range(slot_count):
            bias[h, :, s * tokens : (s + 1) * tokens] = jnp.broadcast_to(
                lowered[:, s : s + 1], (rows, tokens)
            )

    projected, square_sum = own_partial, squares
    for copy in started:
        copy.wait_recv()
    for offset in range(1, lenders):
        projected = projected + q_recv[offset, :, :width]
        square_sum = square_sum + q_recv[offset, :, width : width + 1]
    inverse = lax.rsqrt(square_sum / (act_ref.shape[1] * lenders) + epsilon)
    normed = projected * inverse * head_dim ** (-0.5)
    q_all[me] = jnp.concatenate(
        [normed[:, j * head_dim : (j + 1) * head_dim] for j in range(chunk_heads)], axis=0
    ).astype(bf16)
    for offset in far_first:
        copy = to_lender(1, offset, q_all.at[me], q_all.at[me])
        copy.start()
        started.append(copy)

    step_slots = max(1, min(slot_count, 512 // tokens))
    step = step_slots * tokens
    steps = slot_count // step_slots
    eye = lax.broadcasted_iota(jnp.int32, (chunk_rows, LANES), 0) == lax.broadcasted_iota(
        jnp.int32, (chunk_rows, LANES), 1
    )
    first_line = lax.broadcasted_iota(jnp.int32, (SUBLANES, LANES), 0) == 0
    for h in range(kv_heads):
        chunks = range(h * chunks_per_kv, (h + 1) * chunks_per_kv)
        for source in chunks:

            @pl.when(me != source)
            def _():
                offset = lax.rem(me - source + lenders, lenders)
                to_lender(1, offset, q_all.at[source], q_all.at[source]).wait_recv()

        if h == 0:
            key_copy.wait()
        queries = q_all[chunks.start : chunks.stop].reshape(group * rows, head_dim)
        running = None
        for c in range(steps):
            block = keys[h, c * step_slots : (c + 1) * step_slots].reshape(step, head_dim)
            found = lax.dot_general(
                queries, block, (((1,), (1,)), ((), ())), preferred_element_type=f32
            )
            found = found.reshape(group, rows, step) + bias[h, :, c * step : (c + 1) * step][None]
            found = found.reshape(group * rows, step)
            scores[h, :, c * step : (c + 1) * step] = found
            for t in range(0, step, LANES):
                piece = found[:, t : t + LANES]
                running = piece if running is None else jnp.maximum(running, piece)
        best = jnp.max(running, axis=1, keepdims=True)
        if h == 0:
            value_copy.wait()
        total = None
        gathered = jnp.zeros((group * rows, head_dim), f32)
        for c in range(steps):
            weights = jnp.exp(scores[h, :, c * step : (c + 1) * step] - best)
            for t in range(0, step, LANES):
                piece = weights[:, t : t + LANES]
                total = piece if total is None else total + piece
            block = values[h, c * step_slots : (c + 1) * step_slots].reshape(step, head_dim)
            gathered = gathered + jnp.dot(
                weights.astype(bf16), block, preferred_element_type=f32
            )
        total = jnp.sum(total, axis=1, keepdims=True)
        for j, d in enumerate(chunks):
            lines = slice(j * chunk_rows, (j + 1) * chunk_rows)
            best_line = jnp.sum(jnp.where(eye, best[lines], 0.0), axis=0, keepdims=True)
            total_line = jnp.sum(jnp.where(eye, total[lines], 0.0), axis=0, keepdims=True)
            part_send[d, :chunk_rows, :] = gathered[lines]
            part_send[d, chunk_rows:, :] = jnp.where(first_line, best_line, total_line)
        for d in chunks:

            @pl.when(me != d)
            def _():
                offset = lax.rem(d - me + lenders, lenders)
                to_lender(2, offset, part_send.at[d], part_recv.at[offset]).start()

    part_recv[0] = part_send[me]
    for offset in range(1, lenders):
        copy = to_lender(2, offset, part_send.at[lender_at(offset)], part_recv.at[offset])
        copy.wait_recv()
        started.append(copy)
    bests, totals = [], []
    for offset in range(lenders):
        line = part_recv[offset, chunk_rows : chunk_rows + 1, :]
        bests.append(jnp.sum(jnp.where(eye, line, 0.0), axis=1, keepdims=True))
        line = part_recv[offset, chunk_rows + 1 : chunk_rows + 2, :]
        totals.append(jnp.sum(jnp.where(eye, line, 0.0), axis=1, keepdims=True))
    highest = functools.reduce(jnp.maximum, bests)
    home_total = jnp.zeros((chunk_rows, 1), f32)
    home_value = jnp.zeros((chunk_rows, head_dim), f32)
    for offset in range(lenders):
        factor = jnp.exp(bests[offset] - highest)
        home_total = home_total + totals[offset] * factor
        home_value = home_value + part_recv[offset, :chunk_rows, :] * factor
    att_all[part, me] = (home_value / home_total).astype(bf16)
    att_copies = {}
    for offset in far_first + [0]:
        for step in range(groups):
            if (step, offset) == (0, 0):
                continue
            copy = pltpu.make_async_remote_copy(
                src_ref=att_all.at[part, me],
                dst_ref=att_all.at[part, me],
                send_sem=att_send.at[step, offset],
                recv_sem=att_recv.at[step, offset],
                device_id={"group": group_at(step), "lender": lender_at(offset)},
                device_id_type=MESH,
            )
            copy.start()
            att_copies[step, offset] = copy
    started += att_copies.values()

    product = None
    for offset in range(lenders):
        wo_copies[offset].wait()
        for step in range(groups):
            if (step, offset) != (0, 0):
                att_copies[step, offset].wait_recv()
        source = lender_at(lenders - offset)
        chunks = []
        for g in range(groups):
            chunk = att_all[g, source].astype(f32)
            chunks.append(
                jnp.concatenate(
                    [chunk[j * rows : (j + 1) * rows] for j in range(chunk_heads)], axis=1
                )
            )
        chunk = jnp.concatenate(chunks, axis=0).astype(bf16)
        term = jnp.dot(chunk, wo[offset], preferred_element_type=f32)
        product = term if product is None else product + term

    home_rows = rows // tensors
    part_width = share // tensors
    line_block = lax.broadcasted_iota(jnp.int32, (rows, part_width), 0) // home_rows
    for g in range(groups):
        for d in range(tensors):
            packed = jnp.zeros((rows, part_width), f32)
            for c in range(tensors):
                piece = product[
                    g * rows : (g + 1) * rows, c * part_width : (c + 1) * part_width
                ]
                shift = (c - d) * home_rows % rows
                if shift:
                    piece = pltpu.roll(piece, shift, 0)
                packed = jnp.where(line_block == c, piece, packed)
            sum_send[g, d] = packed
    sum_copies = []
    for step in range(groups):
        for offset in range(tensors):
            if (step, offset) == (0, 0):
                continue
            copy = pltpu.make_async_remote_copy(
                src_ref=sum_send.at[group_at(step), tensor_at(offset)],
                dst_ref=sum_recv.at[part, offset],
                send_sem=tensor_send.at[step, offset],
                recv_sem=tensor_recv.at[step, offset],
                device_id={"group": group_at(step), "tensor": tensor_at(offset)},
                device_id_type=MESH,
            )
            copy.start()
            sum_copies.append(copy)
    started += sum_copies
    sum_recv[part, 0] = sum_send[part, mine]
    for copy in sum_copies:
        copy.wait_recv()
    for g in range(groups):
        result = sum_recv[g, 0]
        for offset in range(1, tensors):
            result = result + sum_recv[g, offset]
        for c in range(tensors):
            at = g * share + c * part_width
            out_ref[:, at : at + part_width] = result[
                c * home_rows : (c + 1) * home_rows
            ].astype(out_ref.dtype)
    for copy in started:
        copy.wait_send()


def fused(
    activations,
    norm_gain,
    w_query,
    w_out,
    key_pool,
    value_block_store,
    block_list,
    block_slot_table,
    kept_len,
):
    groups = lax.axis_size("group")
    lenders, tensors = lax.axis_size("lender"), lax.axis_size("tensor")
    rows, depth = activations.shape
    kv_heads, slot_count, tokens, head_dim = key_pool.shape
    width = w_query.shape[1] // lenders
    out_width = w_out.shape[1]
    chunk_rows = width // head_dim * rows
    group_rows = w_query.shape[1] // head_dim // kv_heads * rows
    share = out_width // groups
    part_width = share // tensors
    f32, bf16 = jnp.float32, jnp.bfloat16
    vmem = pl.BlockSpec(memory_space=pltpu.VMEM)
    hbm = pl.BlockSpec(memory_space=pltpu.HBM)
    return pl.pallas_call(
        functools.partial(fused_kernel, groups, lenders, tensors),
        out_shape=jax.ShapeDtypeStruct((rows // tensors, out_width), bf16),
        in_specs=[hbm] * 9,
        out_specs=vmem,
        scratch_shapes=[
            pltpu.VMEM(activations.shape, bf16),
            pltpu.VMEM(norm_gain.shape, bf16),
            pltpu.VMEM(block_list.shape, jnp.int32),
            pltpu.VMEM(block_slot_table.shape, jnp.int32),
            pltpu.VMEM(kept_len.shape[::-1], jnp.int32),
            pltpu.VMEM((lenders, depth, width), bf16),
            pltpu.VMEM((lenders, width, share), bf16),
            pltpu.VMEM(key_pool.shape, bf16),
            pltpu.VMEM(key_pool.shape, bf16),
            pltpu.VMEM((lenders, rows, width + LANES), f32),
            pltpu.VMEM((lenders, rows, width + LANES), f32),
            pltpu.VMEM((lenders, chunk_rows, head_dim), bf16),
            pltpu.VMEM((kv_heads, rows, slot_count * tokens), f32),
            pltpu.VMEM((kv_heads, group_rows, slot_count * tokens), f32),
            pltpu.VMEM((lenders, chunk_rows + SUBLANES, head_dim), f32),
            pltpu.VMEM((lenders, chunk_rows + SUBLANES, head_dim), f32),
            pltpu.VMEM((groups, lenders, chunk_rows, head_dim), bf16),
            pltpu.VMEM((groups, tensors, rows, part_width), f32),
            pltpu.VMEM((groups, tensors, rows, part_width), f32),
            pltpu.SemaphoreType.DMA((5,)),
            pltpu.SemaphoreType.DMA((lenders,)),
            pltpu.SemaphoreType.DMA((lenders,)),
            pltpu.SemaphoreType.DMA((2,)),
            pltpu.SemaphoreType.DMA((3, lenders)),
            pltpu.SemaphoreType.DMA((3, lenders)),
            pltpu.SemaphoreType.DMA((groups, lenders)),
            pltpu.SemaphoreType.DMA((groups, lenders)),
            pltpu.SemaphoreType.DMA((groups, tensors)),
            pltpu.SemaphoreType.DMA((groups, tensors)),
        ],
        compiler_params=pltpu.CompilerParams(
            collective_id=0, has_side_effects=True, vmem_limit_bytes=48 * 2**20
        ),
        name="decode_attention",
    )(
        *(
            pltpu.with_memory_space_constraint(array, pltpu.HBM)
            for array in (
                activations,
                norm_gain,
                block_list,
                block_slot_table,
                kept_len.T,
                w_query,
                w_out,
                key_pool,
                value_block_store,
            )
        )
    )


def per_device(*arrays):
    activations, _, w_query, w_out, key_pool = arrays[:5]
    lenders, tensors = lax.axis_size("lender"), lax.axis_size("tensor")
    rows = activations.shape[0]
    kv_heads, slot_count, tokens, head_dim = key_pool.shape
    columns, out_width = w_query.shape[1], w_out.shape[1]
    width = columns // lenders
    fits = (
        rows == SUBLANES
        and head_dim == LANES
        and tokens == LANES
        and columns % (lenders * head_dim) == 0
        and columns // kv_heads % max(width, 1) == 0
        and width * rows % (2 * SUBLANES * head_dim) == 0
        and width * rows <= LANES * head_dim
        and rows % tensors == 0
        and out_width % (lax.axis_size("group") * tensors * LANES) == 0
        and slot_count * tokens % 512 == 0
    )
    return (fused if fits else separate_ops)(*arrays)


def solution(mesh):
    in_specs = (
        P("group", "lender"),
        P("lender"),
        P("lender", "tensor"),
        P("tensor", "lender"),
        P("tensor", ("group", "lender"), None, None),
        P("tensor", ("group", "lender"), None, None),
        P("group", "tensor", None),
        P("tensor", "group"),
        P("group", "tensor"),
    )
    out_specs = P(("group", "tensor"), "lender")
    return jax.shard_map(
        per_device, mesh=mesh, in_specs=in_specs, out_specs=out_specs, check_vma=False
    )
```

```python
import functools

import jax
import jax.numpy as jnp
from jax import lax
from jax.experimental import pallas as pl
from jax.experimental.pallas import tpu as pltpu
from jax.sharding import PartitionSpec as P

very_low = -1e30
epsilon = 1e-05


def separate_ops(
    activations,
    norm_gain,
    w_query,
    w_out,
    key_pool,
    value_block_store,
    block_list,
    block_slot_table,
    kept_len,
):
    row_count = activations.shape[0]
    kv_heads = key_pool.shape[0]
    slot_count = key_pool.shape[1]
    head_dim = key_pool.shape[3]
    kept_most = block_list.shape[2]
    features = activations.astype(jnp.float32)
    squares = jnp.sum(features * features, axis=1)
    scaled = (features * norm_gain.astype(jnp.float32)).astype(jnp.bfloat16)
    partial_value = jnp.dot(scaled, w_query, preferred_element_type=jnp.float32)
    projected, square_sum = lax.psum((partial_value, squares), "lender")
    width = features.shape[1] * lax.axis_size("lender")
    inverse = lax.rsqrt(square_sum / width + epsilon)
    query_vectors = (projected * inverse[:, None] * head_dim ** (-0.5)).astype(jnp.bfloat16)
    group_size = query_vectors.shape[1] // (kv_heads * head_dim)
    query_vectors = query_vectors.reshape(row_count, kv_heads, group_size, head_dim)
    slot_lookup_table = jnp.broadcast_to(
        block_slot_table[None], (row_count,) + block_slot_table.shape
    )
    slot_ids = jnp.take_along_axis(slot_lookup_table, block_list, axis=2)
    positions = jnp.arange(kept_most, dtype=jnp.int32)
    is_live = positions[None, None, :] < kept_len[:, :, None]
    local_slot = slot_ids - lax.axis_index("lender") * slot_count
    matches = is_live[..., None] & (
        local_slot[..., None] == jnp.arange(slot_count, dtype=jnp.int32)
    )
    owner_mask = jnp.transpose(jnp.any(matches, axis=2), (1, 2, 0))
    owner_half = owner_mask.astype(jnp.bfloat16)
    owner_full = owner_mask.astype(jnp.float32)
    used_slot = jnp.any(owner_mask, axis=2)
    picked = jnp.einsum(
        "hsr,rhgd->hsgd", owner_half, query_vectors, preferred_element_type=jnp.float32
    ).astype(jnp.bfloat16)
    scores = jnp.einsum("hsgd,hstd->hsgt", picked, key_pool, preferred_element_type=jnp.float32)
    block_best = jnp.max(scores, axis=3)
    spread = jnp.where(owner_mask[..., None], block_best[:, :, None, :], very_low)
    row_best = jnp.max(spread, axis=1)
    slot_best = jnp.max(jnp.where(owner_mask[..., None], row_best[:, None, :, :], very_low), axis=2)
    slot_best = jnp.where(used_slot[..., None], slot_best, 0.0)
    weights_full = jnp.where(
        used_slot[:, :, None, None], jnp.exp(scores - slot_best[..., None]), 0.0
    )
    slot_weight = jnp.sum(weights_full, axis=3)
    slot_value = jnp.einsum(
        "hsgt,hstd->hsgd",
        weights_full.astype(jnp.bfloat16),
        value_block_store,
        preferred_element_type=jnp.float32,
    )
    row_weight = jnp.einsum(
        "hsr,hsg->rhg", owner_full, slot_weight, precision=lax.Precision.HIGHEST
    )
    row_value = jnp.einsum(
        "hsr,hsgd->rhgd", owner_full, slot_value, precision=lax.Precision.HIGHEST
    )
    row_high = jnp.transpose(row_best, (1, 0, 2))
    lenders = lax.axis_size("lender")
    home_rows = row_count // lenders
    came_best, came_weight, came_value = (
        lax.all_to_all(row_high, "lender", split_axis=0, concat_axis=0, tiled=True),
        lax.all_to_all(row_weight, "lender", split_axis=0, concat_axis=0, tiled=True),
        lax.all_to_all(row_value, "lender", split_axis=0, concat_axis=0, tiled=True),
    )
    came_best = came_best.reshape((lenders, home_rows) + came_best.shape[1:])
    came_weight = came_weight.reshape((lenders, home_rows) + came_weight.shape[1:])
    came_value = came_value.reshape((lenders, home_rows) + came_value.shape[1:])
    highest = jnp.max(came_best, axis=0)
    factor = jnp.exp(came_best - highest[None])
    home_weight = jnp.sum(came_weight * factor, axis=0)
    home_value = jnp.sum(came_value * factor[..., None], axis=0)
    home_attended = (
        (home_value / home_weight[..., None]).astype(jnp.bfloat16).reshape(home_rows, -1)
    )
    attended = lax.all_gather(home_attended, "lender", axis=0, tiled=True)
    result = lax.psum_scatter(
        jnp.dot(attended, w_out, preferred_element_type=jnp.float32),
        "tensor",
        scatter_dimension=0,
        tiled=True,
    )
    return result.astype(jnp.bfloat16)


MESH = pl.DeviceIdType.MESH
LANES = 128
SUBLANES = 8


def fused_kernel(
    lenders,
    tensors,
    act_hbm,
    gain_hbm,
    list_hbm,
    table_hbm,
    kept_hbm,
    wq_hbm,
    wo_hbm,
    key_hbm,
    value_hbm,
    out_ref,
    act_ref,
    gain_ref,
    list_ref,
    table_ref,
    kept_ref,
    wq,
    wo,
    keys,
    values,
    q_send,
    q_recv,
    q_all,
    bias,
    scores,
    part_send,
    part_recv,
    att_all,
    sum_send,
    sum_recv,
    small_sem,
    wq_sem,
    wo_sem,
    kv_sem,
    lender_send,
    lender_recv,
    tensor_send,
    tensor_recv,
):
    me = lax.axis_index("lender")
    mine = lax.axis_index("tensor")
    rows = act_ref.shape[0]
    kv_heads, slot_count, tokens, head_dim = keys.shape
    width = wq.shape[2]
    chunk_heads = width // head_dim
    chunk_rows = chunk_heads * rows
    group = wo.shape[0] * chunk_heads // kv_heads
    chunks_per_kv = group // chunk_heads
    kept_most = list_ref.shape[2]
    f32, bf16 = jnp.float32, jnp.bfloat16

    def lender_at(offset):
        return lax.rem(me + offset, lenders)

    far_first = sorted(range(1, lenders), key=lambda offset: abs(2 * offset - lenders))
    small_copies = [
        pltpu.make_async_copy(src, dst, small_sem.at[at])
        for at, (src, dst) in enumerate(
            (
                (act_hbm, act_ref),
                (gain_hbm, gain_ref),
                (list_hbm, list_ref),
                (table_hbm, table_ref),
                (kept_hbm, kept_ref),
            )
        )
    ]
    wq_copies = []
    for offset in far_first + [0]:
        columns = pl.ds(pl.multiple_of(lender_at(offset) * width, width), width)
        wq_copies.append(
            pltpu.make_async_copy(wq_hbm.at[:, columns], wq.at[offset], wq_sem.at[offset])
        )
    key_copy = pltpu.make_async_copy(key_hbm, keys, kv_sem.at[0])
    value_copy = pltpu.make_async_copy(value_hbm, values, kv_sem.at[1])
    wo_copies = []
    for offset in range(lenders):
        source = lender_at(lenders - offset)
        lines = pl.ds(pl.multiple_of(source * width, width), width)
        wo_copies.append(
            pltpu.make_async_copy(wo_hbm.at[lines], wo.at[offset], wo_sem.at[offset])
        )
    for copy in small_copies[:2]:
        copy.start()
    for copy in wq_copies:
        copy.start()

    barrier = pltpu.get_barrier_semaphore()
    for offset in range(1, lenders):
        pl.semaphore_signal(
            barrier, inc=1, device_id={"lender": lender_at(offset)}, device_id_type=MESH
        )
    for offset in range(1, tensors):
        pl.semaphore_signal(
            barrier,
            inc=1,
            device_id={"tensor": lax.rem(mine + offset, tensors)},
            device_id_type=MESH,
        )

    def to_lender(stage, offset, src, dst):
        return pltpu.make_async_remote_copy(
            src_ref=src,
            dst_ref=dst,
            send_sem=lender_send.at[stage, offset],
            recv_sem=lender_recv.at[stage, offset],
            device_id={"lender": lender_at(offset)},
            device_id_type=MESH,
        )

    for copy in small_copies[:2]:
        copy.wait()
    features = act_ref[...].astype(f32)
    squares = jnp.sum(features * features, axis=1, keepdims=True)
    scaled = (features * gain_ref[...].astype(f32).reshape(1, -1)).astype(bf16)

    started = []
    own_partial = None
    for at, offset in enumerate(far_first + [0]):
        wq_copies[at].wait()
        if at == 0:
            for copy in small_copies[2:]:
                copy.start()
        partial = jnp.dot(scaled, wq[offset], preferred_element_type=f32)
        if offset == 0:
            own_partial = partial
            key_copy.start()
            value_copy.start()
            continue
        q_send[offset, :, :width] = partial
        q_send[offset, :, width:] = jnp.broadcast_to(squares, (rows, LANES))
        if at == 0:
            pl.semaphore_wait(barrier, lenders + tensors - 2)
        copy = to_lender(0, offset, q_send.at[offset], q_recv.at[offset])
        copy.start()
        started.append(copy)

    for copy in small_copies[2:]:
        copy.wait()
    blocks = table_ref.shape[1]
    block_ids = lax.broadcasted_iota(jnp.int32, (rows, blocks), 1)
    local_slots = lax.broadcasted_iota(jnp.int32, (slot_count, blocks), 0) + me * slot_count
    row_eye = lax.broadcasted_iota(jnp.int32, (rows, rows), 0) == lax.broadcasted_iota(
        jnp.int32, (rows, rows), 1
    )
    for h in range(kv_heads):
        member = jnp.zeros((rows, blocks), f32)
        listed = list_ref[:, h, :]
        kept = jnp.sum(jnp.where(row_eye, kept_ref[h : h + 1, :], 0), axis=1, keepdims=True)
        for k in range(kept_most):
            hit = (listed[:, k : k + 1] == block_ids) & (kept > k)
            member = jnp.where(hit, 1.0, member)
        holds = jnp.where(table_ref[h : h + 1, :] == local_slots, 1.0, 0.0)
        owner = lax.dot_general(
            member.astype(bf16),
            holds.astype(bf16),
            (((1,), (1,)), ((), ())),
            preferred_element_type=f32,
        )
        lowered = (owner - 1.0) * -very_low
        for s in range(slot_count):
            bias[h, :, s * tokens : (s + 1) * tokens] = jnp.broadcast_to(
                lowered[:, s : s + 1], (rows, tokens)
            )

    projected, square_sum = own_partial, squares
    for copy in started:
        copy.wait_recv()
    for offset in range(1, lenders):
        projected = projected + q_recv[offset, :, :width]
        square_sum = square_sum + q_recv[offset, :, width : width + 1]
    inverse = lax.rsqrt(square_sum / (act_ref.shape[1] * lenders) + epsilon)
    normed = projected * inverse * head_dim ** (-0.5)
    q_all[me] = jnp.concatenate(
        [normed[:, j * head_dim : (j + 1) * head_dim] for j in range(chunk_heads)], axis=0
    ).astype(bf16)
    for offset in far_first:
        copy = to_lender(1, offset, q_all.at[me], q_all.at[me])
        copy.start()
        started.append(copy)
    for copy in wo_copies:
        copy.start()

    step_slots = max(1, min(slot_count, 512 // tokens))
    step = step_slots * tokens
    steps = slot_count // step_slots
    eye = lax.broadcasted_iota(jnp.int32, (chunk_rows, LANES), 0) == lax.broadcasted_iota(
        jnp.int32, (chunk_rows, LANES), 1
    )
    first_line = lax.broadcasted_iota(jnp.int32, (SUBLANES, LANES), 0) == 0
    for h in range(kv_heads):
        chunks = range(h * chunks_per_kv, (h + 1) * chunks_per_kv)
        for source in chunks:

            @pl.when(me != source)
            def _():
                offset = lax.rem(me - source + lenders, lenders)
                to_lender(1, offset, q_all.at[source], q_all.at[source]).wait_recv()

        if h == 0:
            key_copy.wait()
        queries = q_all[chunks.start : chunks.stop].reshape(group * rows, head_dim)
        running = None
        for c in range(steps):
            block = keys[h, c * step_slots : (c + 1) * step_slots].reshape(step, head_dim)
            found = lax.dot_general(
                queries, block, (((1,), (1,)), ((), ())), preferred_element_type=f32
            )
            found = found.reshape(group, rows, step) + bias[h, :, c * step : (c + 1) * step][None]
            found = found.reshape(group * rows, step)
            scores[h, :, c * step : (c + 1) * step] = found
            for t in range(0, step, LANES):
                piece = found[:, t : t + LANES]
                running = piece if running is None else jnp.maximum(running, piece)
        best = jnp.max(running, axis=1, keepdims=True)
        if h == 0:
            value_copy.wait()
        total = None
        gathered = jnp.zeros((group * rows, head_dim), f32)
        for c in range(steps):
            weights = jnp.exp(scores[h, :, c * step : (c + 1) * step] - best)
            for t in range(0, step, LANES):
                piece = weights[:, t : t + LANES]
                total = piece if total is None else total + piece
            block = values[h, c * step_slots : (c + 1) * step_slots].reshape(step, head_dim)
            gathered = gathered + jnp.dot(
                weights.astype(bf16), block, preferred_element_type=f32
            )
        total = jnp.sum(total, axis=1, keepdims=True)
        for j, d in enumerate(chunks):
            lines = slice(j * chunk_rows, (j + 1) * chunk_rows)
            best_line = jnp.sum(jnp.where(eye, best[lines], 0.0), axis=0, keepdims=True)
            total_line = jnp.sum(jnp.where(eye, total[lines], 0.0), axis=0, keepdims=True)
            part_send[d, :chunk_rows, :] = gathered[lines]
            part_send[d, chunk_rows:, :] = jnp.where(first_line, best_line, total_line)
        for d in chunks:

            @pl.when(me != d)
            def _():
                offset = lax.rem(d - me + lenders, lenders)
                to_lender(2, offset, part_send.at[d], part_recv.at[offset]).start()

    part_recv[0] = part_send[me]
    for offset in range(1, lenders):
        copy = to_lender(2, offset, part_send.at[lender_at(offset)], part_recv.at[offset])
        copy.wait_recv()
        started.append(copy)
    bests, totals = [], []
    for offset in range(lenders):
        line = part_recv[offset, chunk_rows : chunk_rows + 1, :]
        bests.append(jnp.sum(jnp.where(eye, line, 0.0), axis=1, keepdims=True))
        line = part_recv[offset, chunk_rows + 1 : chunk_rows + 2, :]
        totals.append(jnp.sum(jnp.where(eye, line, 0.0), axis=1, keepdims=True))
    highest = functools.reduce(jnp.maximum, bests)
    home_total = jnp.zeros((chunk_rows, 1), f32)
    home_value = jnp.zeros((chunk_rows, head_dim), f32)
    for offset in range(lenders):
        factor = jnp.exp(bests[offset] - highest)
        home_total = home_total + totals[offset] * factor
        home_value = home_value + part_recv[offset, :chunk_rows, :] * factor
    att_all[me] = (home_value / home_total).astype(bf16)
    att_copies = {}
    for offset in far_first:
        copy = to_lender(3, offset, att_all.at[me], att_all.at[me])
        copy.start()
        att_copies[offset] = copy
    started += att_copies.values()

    product = None
    for offset in range(lenders):
        wo_copies[offset].wait()
        if offset > 0:
            att_copies[offset].wait_recv()
        chunk = att_all[lender_at(lenders - offset)].astype(f32)
        chunk = jnp.concatenate(
            [chunk[j * rows : (j + 1) * rows] for j in range(chunk_heads)], axis=1
        ).astype(bf16)
        term = jnp.dot(chunk, wo[offset], preferred_element_type=f32)
        product = term if product is None else product + term

    home_rows = rows // tensors
    part_width = product.shape[1] // tensors
    line_block = lax.broadcasted_iota(jnp.int32, (rows, part_width), 0) // home_rows
    for d in range(tensors):
        packed = jnp.zeros((rows, part_width), f32)
        for c in range(tensors):
            piece = product[:, c * part_width : (c + 1) * part_width]
            shift = (c - d) * home_rows % rows
            if shift:
                piece = pltpu.roll(piece, shift, 0)
            packed = jnp.where(line_block == c, piece, packed)
        sum_send[d] = packed
    for offset in range(1, tensors):
        target = lax.rem(mine + offset, tensors)
        copy = pltpu.make_async_remote_copy(
            src_ref=sum_send.at[target],
            dst_ref=sum_recv.at[offset],
            send_sem=tensor_send.at[offset],
            recv_sem=tensor_recv.at[offset],
            device_id={"tensor": target},
            device_id_type=MESH,
        )
        copy.start()
        started.append(copy)
    result = sum_send[mine]
    for copy in started[1 - tensors :] if tensors > 1 else []:
        copy.wait_recv()
    for offset in range(1, tensors):
        result = result + sum_recv[offset]
    for c in range(tensors):
        out_ref[:, c * part_width : (c + 1) * part_width] = result[
            c * home_rows : (c + 1) * home_rows
        ].astype(out_ref.dtype)
    for copy in started:
        copy.wait_send()


def fused(
    activations,
    norm_gain,
    w_query,
    w_out,
    key_pool,
    value_block_store,
    block_list,
    block_slot_table,
    kept_len,
):
    lenders, tensors = lax.axis_size("lender"), lax.axis_size("tensor")
    rows, depth = activations.shape
    kv_heads, slot_count, tokens, head_dim = key_pool.shape
    width = w_query.shape[1] // lenders
    out_width = w_out.shape[1]
    chunk_rows = width // head_dim * rows
    group_rows = w_query.shape[1] // head_dim // kv_heads * rows
    part_width = out_width // tensors
    f32, bf16 = jnp.float32, jnp.bfloat16
    vmem = pl.BlockSpec(memory_space=pltpu.VMEM)
    hbm = pl.BlockSpec(memory_space=pltpu.HBM)
    return pl.pallas_call(
        functools.partial(fused_kernel, lenders, tensors),
        out_shape=jax.ShapeDtypeStruct((rows // tensors, out_width), bf16),
        in_specs=[hbm] * 9,
        out_specs=vmem,
        scratch_shapes=[
            pltpu.VMEM(activations.shape, bf16),
            pltpu.VMEM(norm_gain.shape, bf16),
            pltpu.VMEM(block_list.shape, jnp.int32),
            pltpu.VMEM(block_slot_table.shape, jnp.int32),
            pltpu.VMEM(kept_len.shape[::-1], jnp.int32),
            pltpu.VMEM((lenders, depth, width), bf16),
            pltpu.VMEM((lenders, width, out_width), bf16),
            pltpu.VMEM(key_pool.shape, bf16),
            pltpu.VMEM(key_pool.shape, bf16),
            pltpu.VMEM((lenders, rows, width + LANES), f32),
            pltpu.VMEM((lenders, rows, width + LANES), f32),
            pltpu.VMEM((lenders, chunk_rows, head_dim), bf16),
            pltpu.VMEM((kv_heads, rows, slot_count * tokens), f32),
            pltpu.VMEM((kv_heads, group_rows, slot_count * tokens), f32),
            pltpu.VMEM((lenders, chunk_rows + SUBLANES, head_dim), f32),
            pltpu.VMEM((lenders, chunk_rows + SUBLANES, head_dim), f32),
            pltpu.VMEM((lenders, chunk_rows, head_dim), bf16),
            pltpu.VMEM((tensors, rows, part_width), f32),
            pltpu.VMEM((tensors, rows, part_width), f32),
            pltpu.SemaphoreType.DMA((5,)),
            pltpu.SemaphoreType.DMA((lenders,)),
            pltpu.SemaphoreType.DMA((lenders,)),
            pltpu.SemaphoreType.DMA((2,)),
            pltpu.SemaphoreType.DMA((4, lenders)),
            pltpu.SemaphoreType.DMA((4, lenders)),
            pltpu.SemaphoreType.DMA((tensors,)),
            pltpu.SemaphoreType.DMA((tensors,)),
        ],
        compiler_params=pltpu.CompilerParams(
            collective_id=0, has_side_effects=True, vmem_limit_bytes=48 * 2**20
        ),
        name="decode_attention",
    )(
        *(
            pltpu.with_memory_space_constraint(array, pltpu.HBM)
            for array in (
                activations,
                norm_gain,
                block_list,
                block_slot_table,
                kept_len.T,
                w_query,
                w_out,
                key_pool,
                value_block_store,
            )
        )
    )


def per_device(*arrays):
    activations, _, w_query, w_out, key_pool = arrays[:5]
    lenders, tensors = lax.axis_size("lender"), lax.axis_size("tensor")
    rows = activations.shape[0]
    kv_heads, slot_count, tokens, head_dim = key_pool.shape
    columns, out_width = w_query.shape[1], w_out.shape[1]
    width = columns // lenders
    fits = (
        rows == SUBLANES
        and head_dim == LANES
        and tokens == LANES
        and columns % (lenders * head_dim) == 0
        and columns // kv_heads % max(width, 1) == 0
        and width * rows % (2 * SUBLANES * head_dim) == 0
        and width * rows <= LANES * head_dim
        and rows % tensors == 0
        and out_width % (tensors * LANES) == 0
        and slot_count * tokens % 512 == 0
    )
    return (fused if fits else separate_ops)(*arrays)


def solution(mesh):
    in_specs = (
        P("group", "lender"),
        P("lender"),
        P("lender", "tensor"),
        P("tensor", "lender"),
        P("tensor", ("group", "lender"), None, None),
        P("tensor", ("group", "lender"), None, None),
        P("group", "tensor", None),
        P("tensor", "group"),
        P("group", "tensor"),
    )
    out_specs = P(("group", "tensor"), "lender")
    return jax.shard_map(
        per_device, mesh=mesh, in_specs=in_specs, out_specs=out_specs, check_vma=False
    )
```

```python
import functools

import jax
import jax.numpy as jnp
from jax import lax
from jax.experimental import pallas as pl
from jax.experimental.pallas import tpu as pltpu
from jax.sharding import PartitionSpec as P

very_low = -1e30
epsilon = 1e-05


def separate_ops(
    activations,
    norm_gain,
    w_query,
    w_out,
    key_pool,
    value_block_store,
    block_list,
    block_slot_table,
    kept_len,
):
    row_count = activations.shape[0]
    kv_heads = key_pool.shape[0]
    slot_count = key_pool.shape[1]
    head_dim = key_pool.shape[3]
    kept_most = block_list.shape[2]
    features = activations.astype(jnp.float32)
    squares = jnp.sum(features * features, axis=1)
    scaled = (features * norm_gain.astype(jnp.float32)).astype(jnp.bfloat16)
    partial_value = jnp.dot(scaled, w_query, preferred_element_type=jnp.float32)
    projected, square_sum = lax.psum((partial_value, squares), "lender")
    width = features.shape[1] * lax.axis_size("lender")
    inverse = lax.rsqrt(square_sum / width + epsilon)
    query_vectors = (projected * inverse[:, None] * head_dim ** (-0.5)).astype(jnp.bfloat16)
    group_size = query_vectors.shape[1] // (kv_heads * head_dim)
    query_vectors = query_vectors.reshape(row_count, kv_heads, group_size, head_dim)
    slot_lookup_table = jnp.broadcast_to(
        block_slot_table[None], (row_count,) + block_slot_table.shape
    )
    slot_ids = jnp.take_along_axis(slot_lookup_table, block_list, axis=2)
    positions = jnp.arange(kept_most, dtype=jnp.int32)
    is_live = positions[None, None, :] < kept_len[:, :, None]
    local_slot = slot_ids - lax.axis_index("lender") * slot_count
    matches = is_live[..., None] & (
        local_slot[..., None] == jnp.arange(slot_count, dtype=jnp.int32)
    )
    owner_mask = jnp.transpose(jnp.any(matches, axis=2), (1, 2, 0))
    owner_half = owner_mask.astype(jnp.bfloat16)
    owner_full = owner_mask.astype(jnp.float32)
    used_slot = jnp.any(owner_mask, axis=2)
    picked = jnp.einsum(
        "hsr,rhgd->hsgd", owner_half, query_vectors, preferred_element_type=jnp.float32
    ).astype(jnp.bfloat16)
    scores = jnp.einsum("hsgd,hstd->hsgt", picked, key_pool, preferred_element_type=jnp.float32)
    block_best = jnp.max(scores, axis=3)
    spread = jnp.where(owner_mask[..., None], block_best[:, :, None, :], very_low)
    row_best = jnp.max(spread, axis=1)
    slot_best = jnp.max(jnp.where(owner_mask[..., None], row_best[:, None, :, :], very_low), axis=2)
    slot_best = jnp.where(used_slot[..., None], slot_best, 0.0)
    weights_full = jnp.where(
        used_slot[:, :, None, None], jnp.exp(scores - slot_best[..., None]), 0.0
    )
    slot_weight = jnp.sum(weights_full, axis=3)
    slot_value = jnp.einsum(
        "hsgt,hstd->hsgd",
        weights_full.astype(jnp.bfloat16),
        value_block_store,
        preferred_element_type=jnp.float32,
    )
    row_weight = jnp.einsum(
        "hsr,hsg->rhg", owner_full, slot_weight, precision=lax.Precision.HIGHEST
    )
    row_value = jnp.einsum(
        "hsr,hsgd->rhgd", owner_full, slot_value, precision=lax.Precision.HIGHEST
    )
    row_high = jnp.transpose(row_best, (1, 0, 2))
    lenders = lax.axis_size("lender")
    home_rows = row_count // lenders
    came_best, came_weight, came_value = (
        lax.all_to_all(row_high, "lender", split_axis=0, concat_axis=0, tiled=True),
        lax.all_to_all(row_weight, "lender", split_axis=0, concat_axis=0, tiled=True),
        lax.all_to_all(row_value, "lender", split_axis=0, concat_axis=0, tiled=True),
    )
    came_best = came_best.reshape((lenders, home_rows) + came_best.shape[1:])
    came_weight = came_weight.reshape((lenders, home_rows) + came_weight.shape[1:])
    came_value = came_value.reshape((lenders, home_rows) + came_value.shape[1:])
    highest = jnp.max(came_best, axis=0)
    factor = jnp.exp(came_best - highest[None])
    home_weight = jnp.sum(came_weight * factor, axis=0)
    home_value = jnp.sum(came_value * factor[..., None], axis=0)
    home_attended = (
        (home_value / home_weight[..., None]).astype(jnp.bfloat16).reshape(home_rows, -1)
    )
    attended = lax.all_gather(home_attended, "lender", axis=0, tiled=True)
    result = lax.psum_scatter(
        jnp.dot(attended, w_out, preferred_element_type=jnp.float32),
        "tensor",
        scatter_dimension=0,
        tiled=True,
    )
    return result.astype(jnp.bfloat16)


MESH = pl.DeviceIdType.MESH
LANES = 128
SUBLANES = 8


def fused_kernel(
    lenders,
    tensors,
    act_hbm,
    gain_hbm,
    list_hbm,
    table_hbm,
    kept_hbm,
    wq_hbm,
    wo_hbm,
    key_hbm,
    value_hbm,
    out_ref,
    act_ref,
    gain_ref,
    list_ref,
    table_ref,
    kept_ref,
    wq,
    wo,
    keys,
    values,
    q_send,
    q_recv,
    q_all,
    bias,
    scores,
    part_send,
    part_recv,
    att_all,
    sum_send,
    sum_recv,
    small_sem,
    wq_sem,
    wo_sem,
    kv_sem,
    lender_send,
    lender_recv,
    tensor_send,
    tensor_recv,
):
    me = lax.axis_index("lender")
    mine = lax.axis_index("tensor")
    rows = act_ref.shape[0]
    kv_heads, slot_count, tokens, head_dim = keys.shape
    width = wq.shape[2]
    chunk_heads = width // head_dim
    chunk_rows = chunk_heads * rows
    group = wo.shape[0] * chunk_heads // kv_heads
    chunks_per_kv = group // chunk_heads
    kept_most = list_ref.shape[2]
    f32, bf16 = jnp.float32, jnp.bfloat16

    def lender_at(offset):
        return lax.rem(me + offset, lenders)

    far_first = sorted(range(1, lenders), key=lambda offset: abs(2 * offset - lenders))
    small_copies = [
        pltpu.make_async_copy(src, dst, small_sem.at[at])
        for at, (src, dst) in enumerate(
            (
                (act_hbm, act_ref),
                (gain_hbm, gain_ref),
                (list_hbm, list_ref),
                (table_hbm, table_ref),
                (kept_hbm, kept_ref),
            )
        )
    ]
    wq_copies = []
    for offset in far_first + [0]:
        columns = pl.ds(pl.multiple_of(lender_at(offset) * width, width), width)
        wq_copies.append(
            pltpu.make_async_copy(wq_hbm.at[:, columns], wq.at[offset], wq_sem.at[offset])
        )
    key_copy = pltpu.make_async_copy(key_hbm, keys, kv_sem.at[0])
    value_copy = pltpu.make_async_copy(value_hbm, values, kv_sem.at[1])
    wo_copies = []
    for offset in range(lenders):
        source = lender_at(lenders - offset)
        lines = pl.ds(pl.multiple_of(source * width, width), width)
        wo_copies.append(
            pltpu.make_async_copy(wo_hbm.at[lines], wo.at[offset], wo_sem.at[offset])
        )
    for copy in small_copies[:2]:
        copy.start()
    for copy in wq_copies:
        copy.start()

    barrier = pltpu.get_barrier_semaphore()
    for offset in range(1, lenders):
        pl.semaphore_signal(
            barrier, inc=1, device_id={"lender": lender_at(offset)}, device_id_type=MESH
        )
    for offset in range(1, tensors):
        pl.semaphore_signal(
            barrier,
            inc=1,
            device_id={"tensor": lax.rem(mine + offset, tensors)},
            device_id_type=MESH,
        )

    def to_lender(stage, offset, src, dst):
        return pltpu.make_async_remote_copy(
            src_ref=src,
            dst_ref=dst,
            send_sem=lender_send.at[stage, offset],
            recv_sem=lender_recv.at[stage, offset],
            device_id={"lender": lender_at(offset)},
            device_id_type=MESH,
        )

    for copy in small_copies[:2]:
        copy.wait()
    features = act_ref[...].astype(f32)
    squares = jnp.sum(features * features, axis=1, keepdims=True)
    scaled = (features * gain_ref[...].astype(f32).reshape(1, -1)).astype(bf16)

    started = []
    own_partial = None
    for at, offset in enumerate(far_first + [0]):
        wq_copies[at].wait()
        if at == 0:
            for copy in small_copies[2:]:
                copy.start()
            key_copy.start()
            value_copy.start()
        if at == min(1, lenders - 1):
            for copy in wo_copies:
                copy.start()
        partial = jnp.dot(scaled, wq[offset], preferred_element_type=f32)
        if offset == 0:
            own_partial = partial
            continue
        q_send[offset, :, :width] = partial
        q_send[offset, :, width:] = jnp.broadcast_to(squares, (rows, LANES))
        if at == 0:
            pl.semaphore_wait(barrier, lenders + tensors - 2)
        copy = to_lender(0, offset, q_send.at[offset], q_recv.at[offset])
        copy.start()
        started.append(copy)

    for copy in small_copies[2:]:
        copy.wait()
    blocks = table_ref.shape[1]
    block_ids = lax.broadcasted_iota(jnp.int32, (rows, blocks), 1)
    local_slots = lax.broadcasted_iota(jnp.int32, (slot_count, blocks), 0) + me * slot_count
    row_eye = lax.broadcasted_iota(jnp.int32, (rows, rows), 0) == lax.broadcasted_iota(
        jnp.int32, (rows, rows), 1
    )
    for h in range(kv_heads):
        member = jnp.zeros((rows, blocks), f32)
        listed = list_ref[:, h, :]
        kept = jnp.sum(jnp.where(row_eye, kept_ref[h : h + 1, :], 0), axis=1, keepdims=True)
        for k in range(kept_most):
            hit = (listed[:, k : k + 1] == block_ids) & (kept > k)
            member = jnp.where(hit, 1.0, member)
        holds = jnp.where(table_ref[h : h + 1, :] == local_slots, 1.0, 0.0)
        owner = lax.dot_general(
            member.astype(bf16),
            holds.astype(bf16),
            (((1,), (1,)), ((), ())),
            preferred_element_type=f32,
        )
        lowered = (owner - 1.0) * -very_low
        for s in range(slot_count):
            bias[h, :, s * tokens : (s + 1) * tokens] = jnp.broadcast_to(
                lowered[:, s : s + 1], (rows, tokens)
            )

    projected, square_sum = own_partial, squares
    for copy in started:
        copy.wait_recv()
    for offset in range(1, lenders):
        projected = projected + q_recv[offset, :, :width]
        square_sum = square_sum + q_recv[offset, :, width : width + 1]
    inverse = lax.rsqrt(square_sum / (act_ref.shape[1] * lenders) + epsilon)
    normed = projected * inverse * head_dim ** (-0.5)
    q_all[me] = jnp.concatenate(
        [normed[:, j * head_dim : (j + 1) * head_dim] for j in range(chunk_heads)], axis=0
    ).astype(bf16)
    for offset in far_first:
        copy = to_lender(1, offset, q_all.at[me], q_all.at[me])
        copy.start()
        started.append(copy)

    step_slots = max(1, min(slot_count, 512 // tokens))
    step = step_slots * tokens
    steps = slot_count // step_slots
    eye = lax.broadcasted_iota(jnp.int32, (chunk_rows, LANES), 0) == lax.broadcasted_iota(
        jnp.int32, (chunk_rows, LANES), 1
    )
    first_line = lax.broadcasted_iota(jnp.int32, (SUBLANES, LANES), 0) == 0
    key_copy.wait()
    for copy in started[-len(far_first) :] if far_first else []:
        copy.wait_recv()
    high = []
    for h in range(kv_heads):
        queries = q_all[h * chunks_per_kv : (h + 1) * chunks_per_kv].reshape(
            group * rows, head_dim
        )
        running = None
        for c in range(steps):
            block = keys[h, c * step_slots : (c + 1) * step_slots].reshape(step, head_dim)
            found = lax.dot_general(
                queries, block, (((1,), (1,)), ((), ())), preferred_element_type=f32
            )
            found = found.reshape(group, rows, step) + bias[h, :, c * step : (c + 1) * step][None]
            found = found.reshape(group * rows, step)
            scores[h, :, c * step : (c + 1) * step] = found
            for t in range(0, step, LANES):
                piece = found[:, t : t + LANES]
                running = piece if running is None else jnp.maximum(running, piece)
        high.append(jnp.max(running, axis=1, keepdims=True))
    value_copy.wait()
    for h in range(kv_heads):
        chunks = range(h * chunks_per_kv, (h + 1) * chunks_per_kv)
        best = high[h]
        total = None
        gathered = jnp.zeros((group * rows, head_dim), f32)
        for c in range(steps):
            weights = jnp.exp(scores[h, :, c * step : (c + 1) * step] - best)
            for t in range(0, step, LANES):
                piece = weights[:, t : t + LANES]
                total = piece if total is None else total + piece
            block = values[h, c * step_slots : (c + 1) * step_slots].reshape(step, head_dim)
            gathered = gathered + jnp.dot(
                weights.astype(bf16), block, preferred_element_type=f32
            )
        total = jnp.sum(total, axis=1, keepdims=True)
        for j, d in enumerate(chunks):
            lines = slice(j * chunk_rows, (j + 1) * chunk_rows)
            best_line = jnp.sum(jnp.where(eye, best[lines], 0.0), axis=0, keepdims=True)
            total_line = jnp.sum(jnp.where(eye, total[lines], 0.0), axis=0, keepdims=True)
            part_send[d, :chunk_rows, :] = gathered[lines]
            part_send[d, chunk_rows:, :] = jnp.where(first_line, best_line, total_line)
        for d in chunks:

            @pl.when(me != d)
            def _():
                offset = lax.rem(d - me + lenders, lenders)
                to_lender(2, offset, part_send.at[d], part_recv.at[offset]).start()

    part_recv[0] = part_send[me]
    for offset in range(1, lenders):
        copy = to_lender(2, offset, part_send.at[lender_at(offset)], part_recv.at[offset])
        copy.wait_recv()
        started.append(copy)
    bests, totals = [], []
    for offset in range(lenders):
        line = part_recv[offset, chunk_rows : chunk_rows + 1, :]
        bests.append(jnp.sum(jnp.where(eye, line, 0.0), axis=1, keepdims=True))
        line = part_recv[offset, chunk_rows + 1 : chunk_rows + 2, :]
        totals.append(jnp.sum(jnp.where(eye, line, 0.0), axis=1, keepdims=True))
    highest = functools.reduce(jnp.maximum, bests)
    home_total = jnp.zeros((chunk_rows, 1), f32)
    home_value = jnp.zeros((chunk_rows, head_dim), f32)
    for offset in range(lenders):
        factor = jnp.exp(bests[offset] - highest)
        home_total = home_total + totals[offset] * factor
        home_value = home_value + part_recv[offset, :chunk_rows, :] * factor
    att_all[me] = (home_value / home_total).astype(bf16)
    att_copies = {}
    for offset in far_first:
        copy = to_lender(3, offset, att_all.at[me], att_all.at[me])
        copy.start()
        att_copies[offset] = copy
    started += att_copies.values()

    product = None
    for offset in range(lenders):
        wo_copies[offset].wait()
        if offset > 0:
            att_copies[offset].wait_recv()
        chunk = att_all[lender_at(lenders - offset)].astype(f32)
        chunk = jnp.concatenate(
            [chunk[j * rows : (j + 1) * rows] for j in range(chunk_heads)], axis=1
        ).astype(bf16)
        term = jnp.dot(chunk, wo[offset], preferred_element_type=f32)
        product = term if product is None else product + term

    home_rows = rows // tensors
    part_width = product.shape[1] // tensors
    line_block = lax.broadcasted_iota(jnp.int32, (rows, part_width), 0) // home_rows
    for d in range(tensors):
        packed = jnp.zeros((rows, part_width), f32)
        for c in range(tensors):
            piece = product[:, c * part_width : (c + 1) * part_width]
            shift = (c - d) * home_rows % rows
            if shift:
                piece = pltpu.roll(piece, shift, 0)
            packed = jnp.where(line_block == c, piece, packed)
        sum_send[d] = packed
    for offset in range(1, tensors):
        target = lax.rem(mine + offset, tensors)
        copy = pltpu.make_async_remote_copy(
            src_ref=sum_send.at[target],
            dst_ref=sum_recv.at[offset],
            send_sem=tensor_send.at[offset],
            recv_sem=tensor_recv.at[offset],
            device_id={"tensor": target},
            device_id_type=MESH,
        )
        copy.start()
        started.append(copy)
    result = sum_send[mine]
    for copy in started[1 - tensors :] if tensors > 1 else []:
        copy.wait_recv()
    for offset in range(1, tensors):
        result = result + sum_recv[offset]
    for c in range(tensors):
        out_ref[:, c * part_width : (c + 1) * part_width] = result[
            c * home_rows : (c + 1) * home_rows
        ].astype(out_ref.dtype)
    for copy in started:
        copy.wait_send()


def fused(
    activations,
    norm_gain,
    w_query,
    w_out,
    key_pool,
    value_block_store,
    block_list,
    block_slot_table,
    kept_len,
):
    lenders, tensors = lax.axis_size("lender"), lax.axis_size("tensor")
    rows, depth = activations.shape
    kv_heads, slot_count, tokens, head_dim = key_pool.shape
    width = w_query.shape[1] // lenders
    out_width = w_out.shape[1]
    chunk_rows = width // head_dim * rows
    group_rows = w_query.shape[1] // head_dim // kv_heads * rows
    part_width = out_width // tensors
    f32, bf16 = jnp.float32, jnp.bfloat16
    vmem = pl.BlockSpec(memory_space=pltpu.VMEM)
    hbm = pl.BlockSpec(memory_space=pltpu.HBM)
    return pl.pallas_call(
        functools.partial(fused_kernel, lenders, tensors),
        out_shape=jax.ShapeDtypeStruct((rows // tensors, out_width), bf16),
        in_specs=[hbm] * 9,
        out_specs=vmem,
        scratch_shapes=[
            pltpu.VMEM(activations.shape, bf16),
            pltpu.VMEM(norm_gain.shape, bf16),
            pltpu.VMEM(block_list.shape, jnp.int32),
            pltpu.VMEM(block_slot_table.shape, jnp.int32),
            pltpu.VMEM(kept_len.shape[::-1], jnp.int32),
            pltpu.VMEM((lenders, depth, width), bf16),
            pltpu.VMEM((lenders, width, out_width), bf16),
            pltpu.VMEM(key_pool.shape, bf16),
            pltpu.VMEM(key_pool.shape, bf16),
            pltpu.VMEM((lenders, rows, width + LANES), f32),
            pltpu.VMEM((lenders, rows, width + LANES), f32),
            pltpu.VMEM((lenders, chunk_rows, head_dim), bf16),
            pltpu.VMEM((kv_heads, rows, slot_count * tokens), f32),
            pltpu.VMEM((kv_heads, group_rows, slot_count * tokens), f32),
            pltpu.VMEM((lenders, chunk_rows + SUBLANES, head_dim), f32),
            pltpu.VMEM((lenders, chunk_rows + SUBLANES, head_dim), f32),
            pltpu.VMEM((lenders, chunk_rows, head_dim), bf16),
            pltpu.VMEM((tensors, rows, part_width), f32),
            pltpu.VMEM((tensors, rows, part_width), f32),
            pltpu.SemaphoreType.DMA((5,)),
            pltpu.SemaphoreType.DMA((lenders,)),
            pltpu.SemaphoreType.DMA((lenders,)),
            pltpu.SemaphoreType.DMA((2,)),
            pltpu.SemaphoreType.DMA((4, lenders)),
            pltpu.SemaphoreType.DMA((4, lenders)),
            pltpu.SemaphoreType.DMA((tensors,)),
            pltpu.SemaphoreType.DMA((tensors,)),
        ],
        compiler_params=pltpu.CompilerParams(
            collective_id=0, has_side_effects=True, vmem_limit_bytes=48 * 2**20
        ),
        name="decode_attention",
    )(
        *(
            pltpu.with_memory_space_constraint(array, pltpu.HBM)
            for array in (
                activations,
                norm_gain,
                block_list,
                block_slot_table,
                kept_len.T,
                w_query,
                w_out,
                key_pool,
                value_block_store,
            )
        )
    )


def per_device(*arrays):
    activations, _, w_query, w_out, key_pool = arrays[:5]
    lenders, tensors = lax.axis_size("lender"), lax.axis_size("tensor")
    rows = activations.shape[0]
    kv_heads, slot_count, tokens, head_dim = key_pool.shape
    columns, out_width = w_query.shape[1], w_out.shape[1]
    width = columns // lenders
    fits = (
        rows == SUBLANES
        and head_dim == LANES
        and tokens == LANES
        and columns % (lenders * head_dim) == 0
        and columns // kv_heads % max(width, 1) == 0
        and width * rows % (2 * SUBLANES * head_dim) == 0
        and width * rows <= LANES * head_dim
        and rows % tensors == 0
        and out_width % (tensors * LANES) == 0
        and slot_count * tokens % 512 == 0
    )
    return (fused if fits else separate_ops)(*arrays)


def solution(mesh):
    in_specs = (
        P("group", "lender"),
        P("lender"),
        P("lender", "tensor"),
        P("tensor", "lender"),
        P("tensor", ("group", "lender"), None, None),
        P("tensor", ("group", "lender"), None, None),
        P("group", "tensor", None),
        P("tensor", "group"),
        P("group", "tensor"),
    )
    out_specs = P(("group", "tensor"), "lender")
    return jax.shard_map(
        per_device, mesh=mesh, in_specs=in_specs, out_specs=out_specs, check_vma=False
    )
```
